512 devices in a mesh: dp: 64 (over y, z), rep: 8 (over x, core).
Axes of the slice: x: 4, y: 8, z: 8, core: 2. Of those that a mesh axis runs over, the one named last changes fastest.
Arguments:
- tokens: bfloat16 [11264, 1280], P('dp'), may hold values from -6 to 6
- cotangent: bfloat16 [8192, 1280], P('dp'), may hold values from -16 to 16
- counts: int32 [64, 8], replicated, may hold values from 0 to 96, as said below
- hops: int32 [64, 8], replicated, may hold values from 0 to 3, as said below
- offsets: int32 [64, 8], replicated, may hold values from 0 to 128, as said below
- norm_gain: float32 [1280], replicated, may hold values from 0.1 to 1.9
- qkv_weight: bfloat16 [1280, 3840], P('dp', 'rep'), as said below
- out_weight: bfloat16 [1280, 1280], P('dp', 'rep'), may hold values from -0.15625 to 0.15625
Outputs:
- layer_out: bfloat16 [8192, 1280], P('dp')
- input_grad: bfloat16 [11264, 1280], P('dp')
- grad_qkv: float32 [1280, 3840], P('dp', 'rep')
- grad_out: float32 [1280, 1280], P('dp', 'rep')
- grad_gain: float32 [1280], P('dp')
The draws below stay inside these ranges and needn't reach their ends.
Inputs may be any that keep to these rules, and one draw needn't show every extreme that they name: `counts`: the images of one dp index lie one after another from its first home row and take at most 176 rows; some dp index takes all 176. A slot may hold 0 patches. `hops`: every dp index has exactly two slots with each hop 0 to 3, in an order drawn from the seed. The images that one dp index sends at one hop hold at most 16 patches together and each at most half of 16; both bounds are reached. `offsets`: the images that arrive at a dp index, its own hop 0 images included, fill its 128 work rows exactly, without gaps or intersections. `qkv_weight`: columns head after head, each head's query, key and value columns in that order.
All inputs are finite; a program needn't handle non-finite values.
Results may differ from the reference program's by a relative error of at most 0.018.
Values may be sent and summed in bfloat16 or wider, within the bound.
A program may use at most 64 MiB of HBM per device.

```python
import jax
import jax.numpy as jnp
from jax import lax

D = 1280
HEADS = 16
HEAD = 80
WORK = 128
REACH = 3
SLOT = 16
HOME = 176
IMG_DEV = 8
TOK_WORK = 8192
TOK_HOME = 11264
N_DP = 64


def shuffled(subkey):
    return jax.random.permutation(subkey, IMG_DEV)


def image_moves(key):
    first, second, third, fourth = jax.random.split(key, 4)
    half_slot = SLOT // 2
    devices = jnp.arange(N_DP, dtype=jnp.int32)
    moved = jax.random.randint(first, (N_DP, REACH, 2), 0, half_slot + 1, dtype=jnp.int32)
    busiest = jax.random.randint(second, (), 0, N_DP, dtype=jnp.int32)
    distances = jnp.arange(1, REACH + 1, dtype=jnp.int32)
    into_busiest = (devices[:, None] + distances[None, :]) % N_DP == busiest
    moved = jnp.where(into_busiest[:, :, None], 0, moved)
    moved = jnp.where((devices == busiest)[:, None, None], half_slot, moved)
    sent_totals = jnp.sum(moved, axis=2)
    incoming = jnp.zeros((N_DP,), jnp.int32)
    for distance in range(1, REACH + 1):
        incoming = incoming + jnp.roll(sent_totals[:, distance - 1], distance)
    kept_total = WORK - incoming
    kept_first = jax.random.randint(third, (N_DP,), kept_total // 4, kept_total - kept_total // 4 + 1, dtype=jnp.int32)
    kept_first = jnp.where(devices == busiest, kept_total - kept_total // 4, kept_first)
    kept = jnp.stack([kept_first, kept_total - kept_first], axis=1)
    lengths = jnp.concatenate([kept[:, None, :], moved], axis=1).reshape(N_DP, IMG_DEV)
    hop_order = jnp.repeat(jnp.arange(REACH + 1, dtype=jnp.int32), 2)
    orders = jax.vmap(shuffled)(jax.random.split(fourth, N_DP))
    counts = jnp.take_along_axis(lengths, orders, axis=1).astype(jnp.int32)
    hops = hop_order[orders].astype(jnp.int32)
    all_hops = jnp.arange(REACH + 1, dtype=jnp.int32)
    onehot = (hops[:, :, None] == all_hops[None, None, :]).astype(jnp.int32)
    per_hop = counts[:, :, None] * onehot
    before = jnp.cumsum(per_hop, axis=1) - per_hop
    within = jnp.sum(before * onehot, axis=2)
    hop_totals = jnp.sum(per_hop, axis=1)
    arriving = jnp.stack([jnp.roll(hop_totals[:, distance], distance) for distance in range(REACH + 1)], axis=1)
    base_rows = jnp.cumsum(arriving, axis=1) - arriving
    target_dev = (devices[:, None] + hops) % N_DP
    offsets = (base_rows[target_dev, hops] + within).astype(jnp.int32)
    return (counts, hops, offsets)


def draw_counts(key, part):
    return image_moves(key)[0]


def draw_hops(key, part):
    return image_moves(key)[1]


def draw_offsets(key, part):
    return image_moves(key)[2]


def draw_qkv_weight(key, part):
    key = jax.random.fold_in(key, 11)
    first = jax.random.fold_in(key, 0)
    base = jax.random.truncated_normal(first, -4.0, 4.0, (D, HEADS, 3, HEAD), jnp.float32) * D ** (-0.5)
    return base.reshape(D, HEADS * 3 * HEAD).astype(jnp.bfloat16)


def with_spikes(drawn, own_key, source, target, blocks, factor):
    def block_of(dim):
        return (jnp.arange(drawn.shape[dim]) // (drawn.shape[dim] // blocks)).reshape((-1,) + (1,) * (drawn.ndim - 1 - dim))

    first = jax.random.permutation(own_key, blocks)[block_of(target)]
    far = (block_of(target) + blocks // 2) % blocks
    return jnp.where((block_of(source) == first) | (block_of(source) == far), factor * drawn, drawn)


def level_of(own_key, dims, cuts, smallest, top_value):
    factor_of = 1.0
    for dim, blocks in cuts:
        heights = jax.random.uniform(jax.random.fold_in(jax.random.fold_in(own_key, 6), dim), (blocks,), jnp.float32, smallest / len(cuts), top_value / len(cuts))
        factor_of = factor_of * jnp.repeat(jnp.exp(heights), dims[dim] // blocks).reshape((-1,) + (1,) * (len(dims) - 1 - dim))
    return factor_of


def scatter_about(stream_key, dims, deviation, most, cuts=(), held_as=jnp.bfloat16):
    entries = deviation * jax.random.normal(stream_key, dims, jnp.float32)
    if cuts:
        entries = entries * level_of(stream_key, dims, cuts, -0.22, 0.18)
    return jnp.clip(entries, -most, most).astype(held_as)


def gaussian_with(stream_key, extent, spread, limit, cuts, heavy, held_as=jnp.bfloat16):
    values = spread * jax.random.normal(stream_key, extent, jnp.float32)
    if cuts:
        values = values * level_of(stream_key, extent, cuts, -0.22, 0.18)
    return jnp.clip(with_spikes(values, jax.random.fold_in(stream_key, 3), *heavy), -limit, limit).astype(held_as)


def setup_inputs(seed: int = 0) -> dict:
    streams_of = jax.random.split(jax.random.key(seed), 9)
    return {
        "tokens": scatter_about(streams_of[0], (TOK_HOME, D), 1.0, 6.0, ((0, 64),)),
        "cotangent": gaussian_with(streams_of[1], (TOK_WORK, D), 1.0, 16.0, ((0, 64),), (0, 1, 64, 4.0)),
        "counts": draw_counts(jax.random.fold_in(streams_of[8], 71), 0),
        "hops": draw_hops(jax.random.fold_in(streams_of[8], 71), 0),
        "offsets": draw_offsets(jax.random.fold_in(streams_of[8], 71), 0),
        "norm_gain": jnp.clip(1.0 + 0.18 * jax.random.normal(streams_of[5], (D,), jnp.float32), 0.1, 1.9),
        "qkv_weight": draw_qkv_weight(jax.random.fold_in(streams_of[8], 71), 0),
        "out_weight": scatter_about(streams_of[7], (D, HEADS * HEAD), (HEADS * HEAD) ** -0.5, 0.15625, ((0, 64), (1, 8))),
    }


EPSILON = 1e-06
NEGATIVE = -1e+30

def placement_tables(counts, hops, offsets):
    image_ends = jnp.cumsum(counts, axis=1)
    starts = image_ends - counts
    device_total = counts.shape[0]
    position = jnp.arange(HOME, dtype=jnp.int32)
    inside = (position[None, :, None] >= starts[:, None, :]) & (position[None, :, None] < image_ends[:, None, :])
    live_rows = jnp.any(inside, axis=2)
    devices = jnp.arange(device_total, dtype=jnp.int32)[:, None]
    target_dev = (devices + hops) % device_total
    work_start = target_dev * WORK + offsets
    row_target = lax.optimization_barrier(jnp.sum(jnp.where(inside, work_start[:, None, :] + position[None, :, None] - starts[:, None, :], 0), axis=2))
    image_ident = devices * IMG_DEV + jnp.arange(IMG_DEV, dtype=jnp.int32)[None, :]
    row_image = lax.optimization_barrier(jnp.sum(jnp.where(inside, image_ident[:, None, :], 0), axis=2))
    row_target = jnp.where(live_rows, row_target, device_total * WORK).astype(jnp.int32)
    return (row_target.reshape(-1), row_image.reshape(-1).astype(jnp.int32), live_rows.reshape(-1))

def encoder_layer(patch_rows, images, upstream, norm_gain, qkv_weight, out_weight):
    row_count = patch_rows.shape[0]
    head_count = qkv_weight.shape[1] // (3 * HEAD)
    wide_rows = patch_rows.astype(jnp.float32)
    centred = wide_rows - lax.optimization_barrier(jnp.mean(wide_rows, axis=1, keepdims=True))
    inverse = lax.rsqrt(lax.optimization_barrier(jnp.mean(centred * centred, axis=1, keepdims=True)) + EPSILON)
    normed = centred * inverse
    hidden = (normed * norm_gain).astype(jnp.bfloat16)
    projected_qkv = jnp.dot(hidden, qkv_weight, preferred_element_type=jnp.float32).astype(jnp.bfloat16)
    projected_qkv = projected_qkv.reshape(row_count, head_count, 3, HEAD)
    queries = projected_qkv[:, :, 0].astype(jnp.float32)
    key_part = projected_qkv[:, :, 1].astype(jnp.float32)
    value_part = projected_qkv[:, :, 2].astype(jnp.float32)
    score_scale = HEAD ** (-0.5)
    same_image = images[:, None] == images[None, :]
    scores = jnp.einsum('qhd,khd->hqk', queries, key_part) * score_scale
    scores = jnp.where(same_image[None], scores, NEGATIVE)
    row_max = lax.optimization_barrier(jnp.max(scores, axis=2, keepdims=True))
    exponent = jnp.exp(scores - row_max)
    probs = exponent / lax.optimization_barrier(jnp.sum(exponent, axis=2, keepdims=True))
    probs_low = probs.astype(jnp.bfloat16)
    attended = jnp.einsum('hqk,khd->qhd', probs_low.astype(jnp.float32), value_part).astype(jnp.bfloat16)
    attended = attended.reshape(row_count, head_count * HEAD)
    projected = jnp.dot(attended, out_weight.T, preferred_element_type=jnp.float32)
    layer_rows = (wide_rows + projected).astype(jnp.bfloat16)
    grad_attended = jnp.dot(upstream, out_weight, preferred_element_type=jnp.float32).astype(jnp.bfloat16)
    grad_out = jnp.dot(upstream.T, attended, preferred_element_type=jnp.float32)
    grad_heads = grad_attended.reshape(row_count, head_count, HEAD).astype(jnp.float32)
    grad_probs = jnp.einsum('qhd,khd->hqk', grad_heads, value_part)
    grad_values = jnp.einsum('hqk,qhd->khd', probs_low.astype(jnp.float32), grad_heads).astype(jnp.bfloat16)
    grad_scores = probs * (grad_probs - lax.optimization_barrier(jnp.sum(probs * grad_probs, axis=2, keepdims=True)))
    grad_scores = (grad_scores * score_scale).astype(jnp.bfloat16).astype(jnp.float32)
    grad_queries = jnp.einsum('hqk,khd->qhd', grad_scores, key_part).astype(jnp.bfloat16)
    grad_keys = jnp.einsum('hqk,qhd->khd', grad_scores, queries).astype(jnp.bfloat16)
    grad_mixed = jnp.stack([grad_queries, grad_keys, grad_values], axis=2).reshape(row_count, head_count * 3 * HEAD)
    grad_qkv = jnp.dot(hidden.T, grad_mixed, preferred_element_type=jnp.float32)
    grad_hidden = jnp.dot(grad_mixed, qkv_weight.T, preferred_element_type=jnp.float32)
    grad_gain = lax.optimization_barrier(jnp.sum(grad_hidden * normed, axis=0))
    grad_normed = grad_hidden * norm_gain
    correction = grad_normed - lax.optimization_barrier(jnp.mean(grad_normed, axis=1, keepdims=True)) - normed * lax.optimization_barrier(jnp.mean(grad_normed * normed, axis=1, keepdims=True))
    work_grad = (upstream.astype(jnp.float32) + inverse * correction).astype(jnp.bfloat16)
    return (layer_rows, work_grad, grad_qkv, grad_out, grad_gain)

def reference(tokens, cotangent, counts, hops, offsets, norm_gain, qkv_weight, out_weight):
    row_target, row_image, live_rows = placement_tables(counts, hops, offsets)
    work_total = N_DP * WORK
    work_tokens = jnp.zeros((work_total, D), jnp.bfloat16).at[row_target].set(tokens, mode='drop')
    work_image = jnp.zeros((work_total,), jnp.int32).at[row_target].set(row_image, mode='drop')

    def one_device(totals, device_index):
        first_row = (device_index * WORK).astype(jnp.int32)
        patch_rows = lax.dynamic_slice_in_dim(work_tokens, first_row, WORK, 0)
        images = lax.dynamic_slice_in_dim(work_image, first_row, WORK, 0)
        upstream = lax.dynamic_slice_in_dim(cotangent, first_row, WORK, 0)
        layer_rows, work_grad, grad_qkv, grad_out, grad_gain = encoder_layer(patch_rows, images, upstream, norm_gain, qkv_weight, out_weight)
        totals = (totals[0] + grad_qkv, totals[1] + grad_out, totals[2] + grad_gain)
        return (totals, (layer_rows, work_grad))
    zeros_start = (jnp.zeros((D, HEADS * 3 * HEAD), jnp.float32), jnp.zeros((D, HEADS * HEAD), jnp.float32), jnp.zeros((D,), jnp.float32))
    grad_sums, (layer_blocks, grad_blocks) = lax.scan(one_device, zeros_start, jnp.arange(N_DP, dtype=jnp.int32))
    layer_out = layer_blocks.reshape(work_total, D)
    work_grads = grad_blocks.reshape(work_total, D)
    safe_target = jnp.minimum(row_target, work_total - 1)
    input_grad = jnp.where(live_rows[:, None], work_grads[safe_target], jnp.zeros((), jnp.bfloat16))
    return (layer_out, input_grad, grad_sums[0], grad_sums[1], grad_sums[2])
```

```python
import jax
import jax.numpy as jnp
from jax import lax
from jax.experimental import pallas as pl
from jax.experimental.pallas import tpu as pltpu
from jax.sharding import PartitionSpec as P

MESH = pl.DeviceIdType.MESH
BF16 = jnp.bfloat16
F32 = jnp.float32

D = 1280
HEAD = 80
REACH = 3
SLOT = 16
WORK = 128
HOME = 176
SIDE = 8
REP = 8
ROWS = 20
GROUP = SIDE * ROWS
HALF = GROUP // 2
NEAR = SIDE // 2
IMAGES = 8
EPSILON = 1e-06
NEGATIVE = -1e30
PITCH = 24

TILES = (3, 2)
FIRST = (0, 384)
PACK = (80, 48)


def dot(a, b, ca=1, cb=0):
    return lax.dot_general(a, b, (((ca,), (cb,)), ((), ())), preferred_element_type=F32)


def onehot(match):
    return jnp.where(match, 1.0, 0.0).astype(BF16)


def iota(shape, dim):
    return lax.broadcasted_iota(jnp.int32, shape, dim)


def div20(v):
    return (v * 3277) >> 16


def images_of(counts, hops, offsets, dev):
    found = []
    start = jnp.int32(0)
    sent = [jnp.int32(0)] * (REACH + 1)
    for j in range(IMAGES):
        count, hop, offset = counts[dev, j], hops[dev, j], offsets[dev, j]
        within = jnp.int32(0)
        for level in range(1, REACH + 1):
            same = hop == level
            within = jnp.where(same, (level - 1) * SLOT + sent[level], within)
            sent[level] = sent[level] + jnp.where(same, count, 0)
        found.append((count, hop, offset, start, within))
        start = start + count
    return found


def spans_index(width, spans):
    lane = iota((1, width), 1)
    index = jnp.full((1, width), -1, jnp.int32)
    for lower, length, source in spans:
        inside = (lane >= lower) & (lane < lower + length)
        index = jnp.where(inside, lane + (source - lower), index)
    return index


def steps_of(direction):
    return [
        (distance, half)
        for distance in range(1, NEAR + 1)
        for half in (0, 1)
        if distance < NEAR or half == (1 if direction == 0 else 0)
    ]


STEPS = (steps_of(0), steps_of(1))


def kernel(
    tokens, cotangent, counts, hops, offsets, gain, qkv_w, out_w,
    layer_o, input_o, gq_o, go_o, gg_o,
    stage, own0, own1, parts0, parts1, w0, w1, pick0, pick1, put0, put1, perm,
    slots, arrived, work_s, normed_s, hidden_s, inv_s, both_s, both_t,
    g0, g1, ring0, ring1, back0, back1, heard0, heard1,
    hid_p, hid_r, lay_p, lay_r, work_g, lay_f, back_slots, back_arr, gain_s, gain_r,
    part_sem, ring_sem, token_sem, rep_sem, sum_sem, last_sem,
):
    d = lax.axis_index("dp")
    r = lax.axis_index("rep")
    y = d // SIDE
    z = d % SIDE

    def around(value, step, count):
        return lax.rem(value + (step + count), count)

    def at_y(step):
        return around(y, step, SIDE) * SIDE + z

    def at_z(step):
        return y * SIDE + around(z, step, SIDE)

    def at_dp(step):
        return around(d, step, SIDE * SIDE)

    def at_rep(step):
        return around(r, step, REP)

    pending = []

    def remote(src, dst, sems, dp, rep):
        return pltpu.make_async_remote_copy(
            src_ref=src, dst_ref=dst, send_sem=sems.at[0], recv_sem=sems.at[1],
            device_id=(dp, rep), device_id_type=MESH,
        )

    def send(copy):
        copy.start()
        pending.append(copy)
        return copy

    barrier = pltpu.get_barrier_semaphore()
    partners = (
        [(at_y(o), r) for o in range(1, SIDE)]
        + [(at_z(o), r) for o in range(1, SIDE)]
        + [(d, at_rep(o)) for o in range(1, REP)]
        + [(at_dp(o), r) for o in (1, 2, 3, -1, -2, -3)]
    )
    for partner in partners:
        pl.semaphore_signal(barrier, inc=1, device_id=partner, device_id_type=MESH)

    stage[...] = jnp.zeros_like(stage)
    wide = qkv_w[...].astype(F32)
    wide_out = out_w[...].astype(F32)
    for t in range(3):
        stage[PITCH * t : PITCH * t + ROWS, :] = wide[:, 128 * t : 128 * (t + 1)]
    own0[...] = stage[0 : PACK[0], :].astype(BF16)
    stage[0:ROWS, :] = jnp.concatenate([wide[:, 384:480], wide_out[:, 0:32]], axis=1)
    stage[PITCH : PITCH + ROWS, :] = wide_out[:, 32:160]
    own1[...] = stage[0 : PACK[1], :].astype(BF16)

    mine = images_of(counts, hops, offsets, d)
    out_index = spans_index(
        REACH * SLOT, [(w, jnp.where(h > 0, c, 0), s) for c, h, o, s, w in mine]
    )
    slots[...] = dot(
        onehot(iota((HOME, REACH * SLOT), 0) == out_index), tokens[...], 0, 0
    ).astype(BF16)

    pl.semaphore_wait(barrier, len(partners))

    own = (own0, own1)
    parts = (parts0, parts1)
    first_pos = (z, y)
    second_pos = (y, z)
    first_at = (at_z, at_y)
    second_at = (at_y, at_z)
    part_copies = []
    for o in range(1, SIDE):
        for s in (0, 1):
            part_copies.append(
                send(remote(own[s], parts[s].at[first_pos[s]], part_sem.at[s, o], first_at[s](o), r))
            )
    token_copies = [
        send(
            remote(
                slots.at[pl.ds(SLOT * (h - 1), SLOT)], arrived.at[pl.ds(SLOT * (h - 1), SLOT)],
                token_sem.at[0, h - 1], at_dp(h), r,
            )
        )
        for h in range(1, REACH + 1)
    ]
    for s in (0, 1):
        parts[s][first_pos[s]] = own[s][...]

    picks, puts = (pick0, pick1), (put0, put1)
    for s in (0, 1):
        rows = SIDE * PACK[s]
        lane = iota((1, rows), 1)
        block = (lane * 820) >> 16 if s == 0 else (lane * 1366) >> 16
        inner = lane - block * PACK[s]
        dense = iota((1, GROUP), 1)
        owner = div20(dense)
        for t in range(TILES[s]):
            row = inner - PITCH * t
            target = jnp.where((row >= 0) & (row < ROWS), block * ROWS + row, -1)
            picks[s][t] = onehot(iota((GROUP, rows), 0) == target)
            source = dense + owner * (PACK[s] - ROWS) + PITCH * t
            puts[s][t] = onehot(iota((rows, GROUP), 0) == source)

    work_spans, work_ids = [], []
    senders = [mine] + [
        images_of(counts, hops, offsets, at_dp(-h)) for h in range(1, REACH + 1)
    ]
    lane = iota((1, WORK), 1)
    ident = jnp.zeros((1, WORK), F32)
    for h, sender in enumerate(senders):
        for j, (c, hop, o, s, w) in enumerate(sender):
            length = jnp.where(hop == h, c, 0)
            work_spans.append((o, length, s if h == 0 else HOME + w))
            inside = (lane >= o) & (lane < o + length)
            ident = jnp.where(inside, float(h * IMAGES + j), ident)
    work_index = spans_index(WORK, work_spans)

    for copy in part_copies:
        copy.wait_recv()
    weights = (w0, w1)
    for s in (0, 1):
        block = parts[s][...].reshape(SIDE * PACK[s], 128)
        base = pl.multiple_of(second_pos[s] * GROUP, 16)
        for t in range(TILES[s]):
            weights[s][pl.ds(base, GROUP), 128 * t : 128 * (t + 1)] = dot(
                picks[s][t], block
            ).astype(BF16)

    def gather_copy(s, direction, distance, half):
        sign = 1 if direction == 0 else -1
        at = around(second_pos[s], -sign * (distance - 1), SIDE)
        rows = pl.ds(pl.multiple_of(at * GROUP + half * HALF, 16), HALF)
        number = STEPS[direction].index((distance, half))
        return remote(
            weights[s].at[rows], weights[s].at[rows],
            ring_sem.at[0, s, direction, number], second_at[s](sign), r,
        )

    def gather_step(distance):
        for half in (0, 1):
            for direction in (0, 1):
                if (distance, half) not in STEPS[direction]:
                    continue
                for s in (0, 1):
                    if distance > 1:
                        gather_copy(s, direction, distance - 1, half).wait_recv()
                    send(gather_copy(s, direction, distance, half))

    gather_step(1)

    for copy in token_copies:
        copy.wait_recv()
    work = dot(onehot(iota((HOME, WORK), 0) == work_index), tokens[...], 0, 0) + dot(
        onehot(iota((REACH * SLOT, WORK), 0) + HOME == work_index), arrived[...], 0, 0
    )
    work_s[...] = work.astype(BF16)
    centred = work - jnp.mean(work, axis=1, keepdims=True)
    inverse = lax.rsqrt(jnp.mean(centred * centred, axis=1, keepdims=True) + EPSILON)
    normed = centred * inverse
    normed_s[...] = normed
    inv_s[...] = jnp.broadcast_to(inverse, (WORK, 128))
    hidden_s[...] = (normed * gain[...]).astype(BF16)

    gather_step(2)

    lane = iota((1, D), 1)
    outer = (lane * 6554) >> 20
    inner = lane - outer * GROUP
    middle = div20(inner)
    natural = middle * GROUP + outer * ROWS + (inner - middle * ROWS)
    for b in range(D // 256):
        perm[256 * b : 256 * (b + 1), :] = onehot(iota((256, D), 0) + 256 * b == natural)
    gather_step(3)
    both_s[0:WORK, :] = dot(hidden_s[...], perm[...]).astype(BF16)
    both_s[WORK : 2 * WORK, :] = dot(cotangent[...], perm[...]).astype(BF16)
    gather_step(4)
    both_t[...] = both_s[...].astype(F32).T.astype(BF16)
    hidden_t = hidden_s[...].astype(F32).T.astype(BF16)
    ids = jnp.broadcast_to(ident, (WORK, WORK))
    same_image = ids == ids.T
    for direction in (0, 1):
        for distance, half in STEPS[direction]:
            if (distance + 1, half) not in STEPS[direction]:
                for s in (0, 1):
                    gather_copy(s, direction, distance, half).wait_recv()

    pa = dot(hidden_s[...], w0[...]).astype(BF16)
    pb = dot(both_s[...], w1[...]).astype(BF16)
    proj = jnp.concatenate([pa, pb[0:WORK, 0:128]], axis=1)
    scale = HEAD ** (-0.5)
    pieces, attended = [], []
    for j in (0, 1):
        q, k, v = (
            proj[:, 240 * j + HEAD * i : 240 * j + HEAD * (i + 1)] for i in range(3)
        )
        da = pb[WORK : 2 * WORK, 96 + HEAD * j : 96 + HEAD * (j + 1)]
        scores = jnp.where(same_image, dot(q, k, 1, 1) * scale, NEGATIVE)
        exponent = jnp.exp(scores - jnp.max(scores, axis=1, keepdims=True))
        probs = exponent / jnp.sum(exponent, axis=1, keepdims=True)
        probs_low = probs.astype(BF16)
        attended.append(dot(probs_low, v).astype(BF16))
        grad_probs = dot(da, v, 1, 1)
        grad_v = dot(probs_low, da, 0, 0).astype(BF16)
        grad_s = probs * (grad_probs - jnp.sum(probs * grad_probs, axis=1, keepdims=True))
        grad_s = (grad_s * scale).astype(BF16)
        pieces += [
            dot(grad_s, k).astype(BF16),
            dot(grad_s, q, 0, 0).astype(BF16),
            grad_v,
        ]
    mixed = jnp.concatenate(pieces + attended, axis=1)
    mix0 = mixed[:, 0:384]
    mix1 = mixed[:, 384:640]
    in_qkv = iota((WORK, 256), 1) < 96
    mix1_qkv = jnp.where(in_qkv, mix1, jnp.zeros_like(mix1))
    mix1_att = jnp.where(in_qkv, jnp.zeros_like(mix1), mix1)

    g0[...] = dot(hidden_t, mix0)
    g1[...] = dot(both_t[...], jnp.concatenate([mix1_qkv, mix1_att], axis=0))
    totals = (g0, g1)
    rings = (ring0, ring1)

    def sum_copy(s, direction, distance, half):
        sign = 1 if direction == 0 else -1
        number = STEPS[direction].index((distance, half))
        return remote(
            rings[s].at[direction, distance, half], rings[s].at[direction, distance - 1, half],
            ring_sem.at[1, s, direction, number], second_at[s](sign), r,
        )

    def own_term(s, step, half):
        at = around(second_pos[s], step, SIDE)
        return totals[s][pl.ds(pl.multiple_of(at * GROUP + half * HALF, 16), HALF), :]

    def sum_step(distance):
        for half in (0, 1):
            for direction in (0, 1):
                if (distance, half) not in STEPS[direction]:
                    continue
                sign = 1 if direction == 0 else -1
                for s in (0, 1):
                    total = own_term(s, sign * distance, half)
                    if (distance + 1, half) in STEPS[direction]:
                        sum_copy(s, direction, distance + 1, half).wait_recv()
                        total = total + rings[s][direction, distance, half].astype(F32)
                    rings[s][direction, distance, half] = total.astype(BF16)
                    send(sum_copy(s, direction, distance, half))

    def spread(kind, src, dst):
        copies = []
        for o in range(1, REP):
            rows = pl.ds(pl.multiple_of(at_rep(o) * 16, 16), 16)
            copies.append(
                send(remote(src.at[rows], dst.at[r], rep_sem.at[kind, o], d, at_rep(o)))
            )
        return copies

    my_rows = pl.ds(pl.multiple_of(r * 16, 16), 16)

    def summed(copies, src, dst):
        dst[r] = src[my_rows, :]
        for copy in copies:
            copy.wait_recv()
        total = dst[0].astype(F32)
        for i in range(1, REP):
            total = total + dst[i].astype(F32)
        return total

    def share(kind, ref):
        return [
            send(remote(ref.at[my_rows], ref.at[my_rows], rep_sem.at[kind, o], d, at_rep(o)))
            for o in range(1, REP)
        ]

    sum_step(4)
    turned = dot(mix1_qkv, w1[...], 1, 1).astype(BF16)
    hid_p[...] = (dot(mix0, w0[...], 1, 1) + dot(turned, perm[...])).astype(BF16)
    hid_copies = spread(0, hid_p, hid_r)
    sum_step(3)
    turned = dot(mix1_att, w1[...], 1, 1).astype(BF16)
    lay_p[...] = dot(turned, perm[...]).astype(BF16)
    lay_copies = spread(1, lay_p, lay_r)

    back_index = spans_index(
        REACH * SLOT,
        [
            (w, jnp.where(hop == h, c, 0), o)
            for h in range(1, REACH + 1)
            for c, hop, o, s, w in senders[h]
        ],
    )
    home_index = spans_index(
        HOME, [(s, c, jnp.where(h == 0, o, WORK + w)) for c, h, o, s, w in mine]
    )

    sum_step(2)
    grad_hidden = summed(hid_copies, hid_p, hid_r)
    norm_rows = normed_s[my_rows, :]
    grad_normed = grad_hidden * gain[...]
    correction = (
        grad_normed
        - jnp.mean(grad_normed, axis=1, keepdims=True)
        - norm_rows * jnp.mean(grad_normed * norm_rows, axis=1, keepdims=True)
    )
    work_g[my_rows, :] = (
        cotangent[my_rows, :].astype(F32) + inv_s[my_rows, 0:1] * correction
    ).astype(BF16)
    work_copies = share(2, work_g)

    sum_step(1)
    projected = summed(lay_copies, lay_p, lay_r)
    lay_f[my_rows, :] = (work_s[my_rows, :].astype(F32) + projected).astype(BF16)
    layer_copies = share(3, lay_f)

    for copy in work_copies:
        copy.wait_recv()
    back_slots[...] = dot(
        onehot(iota((WORK, REACH * SLOT), 0) == back_index), work_g[...], 0, 0
    ).astype(BF16)
    back_copies = [
        send(
            remote(
                back_slots.at[pl.ds(SLOT * (h - 1), SLOT)], back_arr.at[pl.ds(SLOT * (h - 1), SLOT)],
                token_sem.at[1, h - 1], at_dp(-h), r,
            )
        )
        for h in range(1, REACH + 1)
    ]

    backs, heards = (back0, back1), (heard0, heard1)
    last_copies = ([], [])
    for s in (0, 1):
        halves = []
        for half in (0, 1):
            total = own_term(s, 0, half)
            for direction in (0, 1):
                sum_copy(s, direction, 1, half).wait_recv()
                total = total + rings[s][direction, 0, half].astype(F32)
            halves.append(total.astype(BF16))
        dense = jnp.concatenate(halves, axis=0)
        spreadout = dot(puts[s][0], dense[:, 0:128])
        for t in range(1, TILES[s]):
            spreadout = spreadout + dot(puts[s][t], dense[:, 128 * t : 128 * (t + 1)])
        backs[s][...] = spreadout.astype(BF16).reshape(SIDE, PACK[s], 128)
        for o in range(1, SIDE):
            to = around(first_pos[s], o, SIDE)
            last_copies[s].append(
                send(remote(backs[s].at[to], heards[s].at[first_pos[s]], part_sem.at[2 + s, o], first_at[s](o), r))
            )
        heards[s][first_pos[s]] = backs[s][first_pos[s]]

    gain_at = iota((ROWS, D), 0) + d * ROWS == iota((ROWS, D), 1)
    own_gain = jnp.sum(jnp.where(gain_at, gain[...], 0.0), axis=1, keepdims=True)

    for copy in back_copies:
        copy.wait_recv()
    input_o[...] = (
        dot(onehot(iota((WORK, HOME), 0) == home_index), work_g[...], 0, 0)
        + dot(onehot(iota((REACH * SLOT, HOME), 0) + WORK == home_index), back_arr[...], 0, 0)
    ).astype(BF16)
    for copy in layer_copies:
        copy.wait_recv()
    layer_o[...] = lay_f[...]

    tiles = []
    for s in (0, 1):
        for copy in last_copies[s]:
            copy.wait_recv()
        total = heards[s][0].astype(F32)
        for i in range(1, SIDE):
            total = total + heards[s][i].astype(F32)
        tiles += [total[PITCH * t : PITCH * t + ROWS, :] for t in range(TILES[s])]
    grad_qkv = jnp.concatenate(tiles[0:3] + [tiles[3][:, 0:96]], axis=1)
    gq_o[...] = grad_qkv
    go_o[...] = jnp.concatenate([tiles[3][:, 96:128], tiles[4]], axis=1)
    share_gain = jnp.sum(grad_qkv * qkv_w[...].astype(F32), axis=1, keepdims=True) / own_gain
    gain_s[...] = jnp.zeros_like(gain_s)
    gain_s[0:ROWS, :] = jnp.broadcast_to(share_gain, (ROWS, 128))
    gain_copies = [
        send(remote(gain_s, gain_r.at[r], sum_sem.at[o], d, at_rep(o)))
        for o in range(1, REP)
    ]
    gain_r[r] = gain_s[...]
    for copy in gain_copies:
        copy.wait_recv()
    total = gain_r[0]
    for i in range(1, REP):
        total = total + gain_r[i]
    diagonal = iota((24, 128), 0) == iota((24, 128), 1)
    gg_o[...] = jnp.sum(jnp.where(diagonal, total, 0.0), axis=0, keepdims=True)[:, 0:ROWS]

    for copy in pending:
        copy.wait_send()


def body(tokens, cotangent, counts, hops, offsets, norm_gain, qkv_weight, out_weight):
    vmem = pl.BlockSpec(memory_space=pltpu.VMEM)
    smem = pl.BlockSpec(memory_space=pltpu.SMEM)
    dma = pltpu.SemaphoreType.DMA
    low = lambda *shape: pltpu.VMEM(shape, BF16)
    wide = lambda *shape: pltpu.VMEM(shape, F32)
    outs = pl.pallas_call(
        kernel,
        out_shape=(
            jax.ShapeDtypeStruct((WORK, D), BF16),
            jax.ShapeDtypeStruct((HOME, D), BF16),
            jax.ShapeDtypeStruct((ROWS, 480), F32),
            jax.ShapeDtypeStruct((ROWS, 160), F32),
            jax.ShapeDtypeStruct((1, ROWS), F32),
        ),
        in_specs=[vmem, vmem, smem, smem, smem, vmem, vmem, vmem],
        out_specs=(vmem,) * 5,
        scratch_shapes=[
            wide(80, 128),
            low(PACK[0], 128), low(PACK[1], 128),
            low(SIDE, PACK[0], 128), low(SIDE, PACK[1], 128),
            low(D, 384), low(D, 256),
            low(3, GROUP, SIDE * PACK[0]), low(2, GROUP, SIDE * PACK[1]),
            low(3, SIDE * PACK[0], GROUP), low(2, SIDE * PACK[1], GROUP),
            low(D, D),
            low(REACH * SLOT, D), low(REACH * SLOT, D),
            low(WORK, D), wide(WORK, D), low(WORK, D), wide(WORK, 128),
            low(2 * WORK, D), low(D, 2 * WORK),
            wide(D, 384), wide(D, 256),
            low(2, NEAR + 1, 2, HALF, 384), low(2, NEAR + 1, 2, HALF, 256),
            low(SIDE, PACK[0], 128), low(SIDE, PACK[1], 128),
            low(SIDE, PACK[0], 128), low(SIDE, PACK[1], 128),
            low(WORK, D), low(REP, 16, D), low(WORK, D), low(REP, 16, D),
            low(WORK, D), low(WORK, D),
            low(REACH * SLOT, D), low(REACH * SLOT, D),
            wide(24, 128), wide(REP, 24, 128),
            dma((4, SIDE, 2)),
            dma((2, 2, 2, 7, 2)),
            dma((2, REACH, 2)),
            dma((4, REP, 2)),
            dma((REP, 2)),
            dma((1,)),
        ],
        compiler_params=pltpu.CompilerParams(
            collective_id=0, has_side_effects=True, vmem_limit_bytes=50 * 1024 * 1024
        ),
        name="layer",
    )(
        tokens, cotangent, counts, hops, offsets,
        norm_gain.reshape(1, D), qkv_weight, out_weight,
    )
    layer_out, input_grad, grad_qkv, grad_out, grad_gain = outs
    return (layer_out, input_grad, grad_qkv, grad_out, grad_gain.reshape(ROWS))


def solution(mesh):
    return jax.shard_map(
        body,
        mesh=mesh,
        in_specs=(P("dp", None), P("dp", None), P(), P(), P(), P(), P("dp", "rep"), P("dp", "rep")),
        out_specs=(P("dp", None), P("dp", None), P("dp", "rep"), P("dp", "rep"), P("dp")),
        check_vma=False,
    )
```

```python
import jax
import jax.numpy as jnp
from jax import lax
from jax.experimental import pallas as pl
from jax.experimental.pallas import tpu as pltpu
from jax.sharding import PartitionSpec as P

MESH = pl.DeviceIdType.MESH
BF16 = jnp.bfloat16
F32 = jnp.float32

D = 1280
HEAD = 80
REACH = 3
SLOT = 16
WORK = 128
HOME = 176
SIDE = 8
REP = 8
ROWS = 20
GROUP = SIDE * ROWS
NEAR = SIDE // 2
IMAGES = 8
EPSILON = 1e-06
NEGATIVE = -1e30
PITCH = 24

TILES = (3, 2)
FIRST = (0, 384)
PACK = (80, 48)


def dot(a, b, ca=1, cb=0):
    return lax.dot_general(a, b, (((ca,), (cb,)), ((), ())), preferred_element_type=F32)


def onehot(match):
    return jnp.where(match, 1.0, 0.0).astype(BF16)


def iota(shape, dim):
    return lax.broadcasted_iota(jnp.int32, shape, dim)


def div20(v):
    return (v * 3277) >> 16


def images_of(counts, hops, offsets, dev):
    found = []
    start = jnp.int32(0)
    sent = [jnp.int32(0)] * (REACH + 1)
    for j in range(IMAGES):
        count, hop, offset = counts[j, dev], hops[j, dev], offsets[j, dev]
        within = jnp.int32(0)
        for level in range(1, REACH + 1):
            same = hop == level
            within = jnp.where(same, (level - 1) * SLOT + sent[level], within)
            sent[level] = sent[level] + jnp.where(same, count, 0)
        found.append((count, hop, offset, start, within))
        start = start + count
    return found


def spans_index(width, spans):
    lane = iota((1, width), 1)
    index = jnp.full((1, width), -1, jnp.int32)
    for lower, length, source in spans:
        inside = (lane >= lower) & (lane < lower + length)
        index = jnp.where(inside, lane + (source - lower), index)
    return index


FAR = (((80, 48), (128, 32)), ((0, 48), (48, 32)))
PIECES = (FAR[0] + ((0, 80),), FAR[1] + ((80, 80),))


def steps_of(direction):
    return [
        (distance, piece)
        for distance in range(1, NEAR + 1)
        for piece in PIECES[direction]
        if distance < NEAR or piece in FAR[direction]
    ]


STEPS = (steps_of(0), steps_of(1))


def kernel(
    tokens_h, cotangent_h, counts_h, hops_h, offsets_h, gain_h, qkv_h, out_h,
    layer_h, input_h, gq_h, go_h, gg_h,
    tokens, cotangent, counts, hops, offsets, gain_v, qkv_w, out_w,
    input_o, gq_o, go_o, gg_o,
    stage, own0, own1, parts0, parts1, w0, w1, pick0, pick1, put0, put1, perm,
    slots, arrived, work_s, normed_s, hidden_s, inv_s, both_s, both_t,
    g0, g1, ring0, ring1, back0, back1, heard0, heard1,
    hid_p, hid_r, lay_p, lay_r, work_g, lay_f, back_slots, back_arr, gain_s, gain_r,
    part_sem, ring_sem, token_sem, rep_sem, sum_sem, in_sem, out_sem,
):
    d = lax.axis_index("dp")
    r = lax.axis_index("rep")
    y = d // SIDE
    z = d % SIDE

    def around(value, step, count):
        return lax.rem(value + (step + count), count)

    def at_y(step):
        return around(y, step, SIDE) * SIDE + z

    def at_z(step):
        return y * SIDE + around(z, step, SIDE)

    def at_dp(step):
        return around(d, step, SIDE * SIDE)

    def at_rep(step):
        return around(r, step, REP)

    sent = {}

    def remote(src, dst, sems, dp, rep):
        return pltpu.make_async_remote_copy(
            src_ref=src, dst_ref=dst, send_sem=sems.at[0], recv_sem=sems.at[1],
            device_id=(dp, rep), device_id_type=MESH,
        )

    def send(key, copy):
        copy.start()
        sent[key] = copy

    def got(key):
        sent[key].wait_recv()

    barrier = pltpu.get_barrier_semaphore()
    partners = (
        [(at_y(o), r) for o in range(1, SIDE)]
        + [(at_z(o), r) for o in range(1, SIDE)]
        + [(d, at_rep(o)) for o in range(1, REP)]
        + [(at_dp(o), r) for o in (1, 2, 3, -1, -2, -3)]
    )
    for partner in partners:
        pl.semaphore_signal(barrier, inc=1, device_id=partner, device_id_type=MESH)

    loads = [
        pltpu.make_async_copy(src, dst, in_sem.at[i])
        for i, (src, dst) in enumerate(
            (
                (qkv_h, qkv_w), (out_h, out_w), (counts_h, counts), (hops_h, hops),
                (offsets_h, offsets), (tokens_h, tokens), (gain_h, gain_v), (cotangent_h, cotangent),
            )
        )
    ]
    for load in loads:
        load.start()

    stage[...] = jnp.zeros_like(stage)
    for load in loads[0:2]:
        load.wait()
    wide = qkv_w[...].astype(F32)
    wide_out = out_w[...].astype(F32)
    for t in range(3):
        stage[PITCH * t : PITCH * t + ROWS, :] = wide[:, 128 * t : 128 * (t + 1)]
    own0[...] = stage[0 : PACK[0], :].astype(BF16)
    stage[0:ROWS, :] = jnp.concatenate([wide[:, 384:480], wide_out[:, 0:32]], axis=1)
    stage[PITCH : PITCH + ROWS, :] = wide_out[:, 32:160]
    own1[...] = stage[0 : PACK[1], :].astype(BF16)

    pl.semaphore_wait(barrier, len(partners))

    own = (own0, own1)
    parts = (parts0, parts1)
    first_pos = (z, y)
    second_pos = (y, z)
    first_at = (at_z, at_y)
    second_at = (at_y, at_z)
    for o in range(1, SIDE):
        for s in (0, 1):
            send(
                ("part", s, o),
                remote(own[s], parts[s].at[first_pos[s]], part_sem.at[s, o], first_at[s](o), r),
            )
    for load in loads[2:6]:
        load.wait()
    mine = images_of(counts, hops, offsets, d)
    out_index = spans_index(
        REACH * SLOT, [(w, jnp.where(h > 0, c, 0), s) for c, h, o, s, w in mine]
    )
    slots[...] = dot(
        onehot(iota((HOME, REACH * SLOT), 0) == out_index), tokens[...], 0, 0
    ).astype(BF16)
    for h in range(1, REACH + 1):
        rows = pl.ds(SLOT * (h - 1), SLOT)
        send(
            ("token", h),
            remote(slots.at[rows], arrived.at[rows], token_sem.at[0, h - 1], at_dp(h), r),
        )
    for s in (0, 1):
        parts[s][first_pos[s]] = own[s][...]

    picks, puts = (pick0, pick1), (put0, put1)
    for s in (0, 1):
        rows = SIDE * PACK[s]
        lane = iota((1, rows), 1)
        block = (lane * 820) >> 16 if s == 0 else (lane * 1366) >> 16
        inner = lane - block * PACK[s]
        dense = iota((1, GROUP), 1)
        owner = div20(dense)
        for t in range(TILES[s]):
            row = inner - PITCH * t
            target = jnp.where((row >= 0) & (row < ROWS), block * ROWS + row, -1)
            picks[s][t] = onehot(iota((GROUP, rows), 0) == target)
            source = dense + owner * (PACK[s] - ROWS) + PITCH * t
            puts[s][t] = onehot(iota((rows, GROUP), 0) == source)

    work_spans, work_ids = [], []
    senders = [mine] + [
        images_of(counts, hops, offsets, at_dp(-h)) for h in range(1, REACH + 1)
    ]
    lane = iota((1, WORK), 1)
    ident = jnp.zeros((1, WORK), F32)
    for h, sender in enumerate(senders):
        for j, (c, hop, o, s, w) in enumerate(sender):
            length = jnp.where(hop == h, c, 0)
            work_spans.append((o, length, s if h == 0 else HOME + w))
            inside = (lane >= o) & (lane < o + length)
            ident = jnp.where(inside, float(h * IMAGES + j), ident)
    work_index = spans_index(WORK, work_spans)

    for o in range(1, SIDE):
        for s in (0, 1):
            got(("part", s, o))
    weights = (w0, w1)
    for s in (0, 1):
        block = parts[s][...].reshape(SIDE * PACK[s], 128)
        base = pl.multiple_of(second_pos[s] * GROUP, 16)
        for t in range(TILES[s]):
            weights[s][pl.ds(base, GROUP), 128 * t : 128 * (t + 1)] = dot(
                picks[s][t], block
            ).astype(BF16)

    def gather_copy(s, direction, distance, piece):
        sign = 1 if direction == 0 else -1
        at = around(second_pos[s], -sign * (distance - 1), SIDE)
        rows = pl.ds(pl.multiple_of(at * GROUP + piece[0], 16), piece[1])
        number = STEPS[direction].index((distance, piece))
        return remote(
            weights[s].at[rows], weights[s].at[rows],
            ring_sem.at[0, s, direction, number], second_at[s](sign), r,
        )

    def gather_step(distance):
        for number in range(3 if distance < NEAR else 2):
            for direction in (0, 1):
                piece = PIECES[direction][number]
                for s in (0, 1):
                    if distance > 1:
                        got(("gather", s, direction, distance - 1, piece))
                    send(
                        ("gather", s, direction, distance, piece),
                        gather_copy(s, direction, distance, piece),
                    )

    gather_step(1)

    for load in loads[6:8]:
        load.wait()
    gain = gain_v[...].reshape(1, D)
    for h in range(1, REACH + 1):
        got(("token", h))
    work = dot(onehot(iota((HOME, WORK), 0) == work_index), tokens[...], 0, 0) + dot(
        onehot(iota((REACH * SLOT, WORK), 0) + HOME == work_index), arrived[...], 0, 0
    )
    work_s[...] = work.astype(BF16)
    centred = work - jnp.mean(work, axis=1, keepdims=True)
    inverse = lax.rsqrt(jnp.mean(centred * centred, axis=1, keepdims=True) + EPSILON)
    normed = centred * inverse
    normed_s[...] = normed
    inv_s[...] = jnp.broadcast_to(inverse, (WORK, 128))
    hidden_s[...] = (normed * gain).astype(BF16)

    gather_step(2)

    lane = iota((1, D), 1)
    outer = (lane * 6554) >> 20
    inner = lane - outer * GROUP
    middle = div20(inner)
    natural = middle * GROUP + outer * ROWS + (inner - middle * ROWS)
    for b in range(D // 256):
        perm[256 * b : 256 * (b + 1), :] = onehot(iota((256, D), 0) + 256 * b == natural)
    gather_step(3)
    both_s[0:WORK, :] = dot(hidden_s[...], perm[...]).astype(BF16)
    both_s[WORK : 2 * WORK, :] = dot(cotangent[...], perm[...]).astype(BF16)
    gather_step(4)
    both_t[...] = both_s[...].astype(F32).T.astype(BF16)
    hidden_t = hidden_s[...].astype(F32).T.astype(BF16)
    ids = jnp.broadcast_to(ident, (WORK, WORK))
    same_image = ids == ids.T
    for direction in (0, 1):
        for distance, piece in STEPS[direction]:
            if (distance + 1, piece) not in STEPS[direction]:
                for s in (0, 1):
                    got(("gather", s, direction, distance, piece))

    pa = dot(hidden_s[...], w0[...]).astype(BF16)
    pb = dot(both_s[...], w1[...]).astype(BF16)
    proj = jnp.concatenate([pa, pb[0:WORK, 0:128]], axis=1)
    scale = HEAD ** (-0.5)
    pieces, attended = [], []
    for j in (0, 1):
        q, k, v = (
            proj[:, 240 * j + HEAD * i : 240 * j + HEAD * (i + 1)] for i in range(3)
        )
        da = pb[WORK : 2 * WORK, 96 + HEAD * j : 96 + HEAD * (j + 1)]
        scores = jnp.where(same_image, dot(q, k, 1, 1) * scale, NEGATIVE)
        exponent = jnp.exp(scores - jnp.max(scores, axis=1, keepdims=True))
        probs = exponent / jnp.sum(exponent, axis=1, keepdims=True)
        probs_low = probs.astype(BF16)
        attended.append(dot(probs_low, v).astype(BF16))
        grad_probs = dot(da, v, 1, 1)
        grad_v = dot(probs_low, da, 0, 0).astype(BF16)
        grad_s = probs * (grad_probs - jnp.sum(probs * grad_probs, axis=1, keepdims=True))
        grad_s = (grad_s * scale).astype(BF16)
        pieces += [
            dot(grad_s, k).astype(BF16),
            dot(grad_s, q, 0, 0).astype(BF16),
            grad_v,
        ]
    mixed = jnp.concatenate(pieces + attended, axis=1)
    mix0 = mixed[:, 0:384]
    mix1 = mixed[:, 384:640]
    in_qkv = iota((WORK, 256), 1) < 96
    mix1_qkv = jnp.where(in_qkv, mix1, jnp.zeros_like(mix1))
    mix1_att = jnp.where(in_qkv, jnp.zeros_like(mix1), mix1)

    g0[...] = dot(hidden_t, mix0)
    g1[...] = dot(both_t[...], jnp.concatenate([mix1_qkv, mix1_att], axis=0))
    totals = (g0, g1)
    rings = (ring0, ring1)

    def sum_copy(s, direction, distance, piece):
        sign = 1 if direction == 0 else -1
        number = STEPS[direction].index((distance, piece))
        rows = pl.ds(*piece)
        return remote(
            rings[s].at[direction, distance, rows], rings[s].at[direction, distance - 1, rows],
            ring_sem.at[1, s, direction, number], second_at[s](sign), r,
        )

    def own_term(s, step, piece):
        at = around(second_pos[s], step, SIDE)
        return totals[s][pl.ds(pl.multiple_of(at * GROUP + piece[0], 16), piece[1]), :]

    def sum_step(distance):
        for number in range(3 if distance < NEAR else 2):
            for direction in (0, 1):
                piece = PIECES[direction][number]
                rows = pl.ds(*piece)
                sign = 1 if direction == 0 else -1
                for s in (0, 1):
                    total = own_term(s, sign * distance, piece)
                    if (distance + 1, piece) in STEPS[direction]:
                        got(("sum", s, direction, distance + 1, piece))
                        total = total + rings[s][direction, distance, rows].astype(F32)
                    rings[s][direction, distance, rows] = total.astype(BF16)
                    send(
                        ("sum", s, direction, distance, piece),
                        sum_copy(s, direction, distance, piece),
                    )

    def spread(kind, src, dst):
        for o in range(1, REP):
            rows = pl.ds(pl.multiple_of(at_rep(o) * 16, 16), 16)
            send(
                ("rep", kind, o),
                remote(src.at[rows], dst.at[r], rep_sem.at[kind, o], d, at_rep(o)),
            )

    my_rows = pl.ds(pl.multiple_of(r * 16, 16), 16)

    def all_got(kind):
        for o in range(1, REP):
            got(("rep", kind, o))

    def summed(kind, src, dst):
        dst[r] = src[my_rows, :]
        all_got(kind)
        total = dst[0].astype(F32)
        for i in range(1, REP):
            total = total + dst[i].astype(F32)
        return total

    def share(kind, ref):
        for o in range(1, REP):
            send(
                ("rep", kind, o),
                remote(ref.at[my_rows], ref.at[my_rows], rep_sem.at[kind, o], d, at_rep(o)),
            )

    sum_step(4)
    turned = dot(mix1_qkv, w1[...], 1, 1).astype(BF16)
    hid_p[...] = (dot(mix0, w0[...], 1, 1) + dot(turned, perm[...])).astype(BF16)
    spread(0, hid_p, hid_r)
    sum_step(3)
    turned = dot(mix1_att, w1[...], 1, 1).astype(BF16)
    lay_p[...] = dot(turned, perm[...]).astype(BF16)
    spread(1, lay_p, lay_r)

    back_index = spans_index(
        REACH * SLOT,
        [
            (w, jnp.where(hop == h, c, 0), o)
            for h in range(1, REACH + 1)
            for c, hop, o, s, w in senders[h]
        ],
    )
    home_index = spans_index(
        HOME, [(s, c, jnp.where(h == 0, o, WORK + w)) for c, h, o, s, w in mine]
    )

    sum_step(2)
    grad_hidden = summed(0, hid_p, hid_r)
    norm_rows = normed_s[my_rows, :]
    grad_normed = grad_hidden * gain
    correction = (
        grad_normed
        - jnp.mean(grad_normed, axis=1, keepdims=True)
        - norm_rows * jnp.mean(grad_normed * norm_rows, axis=1, keepdims=True)
    )
    work_g[my_rows, :] = (
        cotangent[my_rows, :].astype(F32) + inv_s[my_rows, 0:1] * correction
    ).astype(BF16)
    share(2, work_g)
    row_gain = jnp.sum(grad_hidden * norm_rows, axis=0, keepdims=True)
    gain_s[...] = jnp.zeros_like(gain_s)
    for t in range(D // 128):
        gain_s[0, t : t + 1, :] = row_gain[:, 128 * t : 128 * (t + 1)]

    gain_at = (
        (r, lambda o: (d, at_rep(o))),
        (y, lambda o: (at_y(o), r)),
        (z, lambda o: (at_z(o), r)),
    )

    def send_gain(level):
        me, peer = gain_at[level]
        for o in range(1, SIDE):
            send(
                ("gain", level, o),
                remote(gain_s.at[level], gain_r.at[level, me], sum_sem.at[level, o], *peer(o)),
            )
        gain_r[level, me] = gain_s[level]

    def sum_gain(level):
        for o in range(1, SIDE):
            got(("gain", level, o))
        total = gain_r[level, 0]
        for i in range(1, SIDE):
            total = total + gain_r[level, i]
        return total

    send_gain(0)

    sum_step(1)
    all_got(2)
    back_slots[...] = dot(
        onehot(iota((WORK, REACH * SLOT), 0) == back_index), work_g[...], 0, 0
    ).astype(BF16)
    for h in range(1, REACH + 1):
        rows = pl.ds(SLOT * (h - 1), SLOT)
        send(
            ("back", h),
            remote(back_slots.at[rows], back_arr.at[rows], token_sem.at[1, h - 1], at_dp(-h), r),
        )

    gain_s[1] = sum_gain(0)
    send_gain(1)

    projected = summed(1, lay_p, lay_r)
    lay_f[my_rows, :] = (work_s[my_rows, :].astype(F32) + projected).astype(BF16)
    share(3, lay_f)

    backs, heards = (back0, back1), (heard0, heard1)
    for s in (0, 1):
        for direction in (0, 1):
            for piece in PIECES[direction]:
                got(("sum", s, direction, 1, piece))
        total = own_term(s, 0, (0, GROUP))
        for direction in (0, 1):
            total = total + rings[s][direction, 0].astype(F32)
        dense = total.astype(BF16)
        spreadout = dot(puts[s][0], dense[:, 0:128])
        for t in range(1, TILES[s]):
            spreadout = spreadout + dot(puts[s][t], dense[:, 128 * t : 128 * (t + 1)])
        backs[s][...] = spreadout.astype(BF16).reshape(SIDE, PACK[s], 128)
        for o in range(1, SIDE):
            to = around(first_pos[s], o, SIDE)
            send(
                ("last", s, o),
                remote(backs[s].at[to], heards[s].at[first_pos[s]], part_sem.at[2 + s, o], first_at[s](o), r),
            )
        heards[s][first_pos[s]] = backs[s][first_pos[s]]

    gain_s[2] = sum_gain(1)
    send_gain(2)

    stores = []

    def store(src, dst):
        copy = pltpu.make_async_copy(src, dst, out_sem.at[len(stores)])
        copy.start()
        stores.append(copy)

    for h in range(1, REACH + 1):
        got(("back", h))
    input_o[...] = (
        dot(onehot(iota((WORK, HOME), 0) == home_index), work_g[...], 0, 0)
        + dot(onehot(iota((REACH * SLOT, HOME), 0) + WORK == home_index), back_arr[...], 0, 0)
    ).astype(BF16)
    store(input_o, input_h)
    all_got(3)
    store(lay_f, layer_h)

    tiles = []
    for s in (0, 1):
        for o in range(1, SIDE):
            got(("last", s, o))
        total = heards[s][0].astype(F32)
        for i in range(1, SIDE):
            total = total + heards[s][i].astype(F32)
        tiles += [total[PITCH * t : PITCH * t + ROWS, :] for t in range(TILES[s])]
    grad_qkv = jnp.concatenate(tiles[0:3] + [tiles[3][:, 0:96]], axis=1)
    gq_o[...] = grad_qkv
    go_o[...] = jnp.concatenate([tiles[3][:, 96:128], tiles[4]], axis=1)
    store(gq_o, gq_h)
    store(go_o, go_h)

    total = sum_gain(2)
    row = jnp.concatenate([total[t : t + 1, :] for t in range(D // 128)], axis=1)
    row = pltpu.roll(jnp.broadcast_to(row, (8, D)), lax.rem(D - ROWS * d, D), 1)
    gg_o[...] = row[0:1, 0:ROWS]
    store(gg_o, gg_h)

    for copy in stores:
        copy.wait()
    for copy in sent.values():
        copy.wait_send()


def finish(*refs):
    held, outs, rooms, sems = refs[0:5], refs[5:10], refs[10:15], refs[15]
    loads = [pltpu.make_async_copy(h, v, sems.at[0, i]) for i, (h, v) in enumerate(zip(held, rooms))]
    stores = [pltpu.make_async_copy(v, o, sems.at[1, i]) for i, (v, o) in enumerate(zip(rooms, outs))]
    for load in loads:
        load.start()
    for load, store in zip(loads, stores):
        load.wait()
        store.start()
    for store in stores:
        store.wait()


def body(tokens, cotangent, counts, hops, offsets, norm_gain, qkv_weight, out_weight):
    outside = pl.BlockSpec(memory_space=pl.ANY)
    dma = pltpu.SemaphoreType.DMA
    low = lambda *shape: pltpu.VMEM(shape, BF16)
    wide = lambda *shape: pltpu.VMEM(shape, F32)
    table = pltpu.SMEM((IMAGES, SIDE * SIDE), jnp.int32)
    shapes = (
        jax.ShapeDtypeStruct((WORK, D), BF16),
        jax.ShapeDtypeStruct((HOME, D), BF16),
        jax.ShapeDtypeStruct((ROWS, 480), F32),
        jax.ShapeDtypeStruct((ROWS, 160), F32),
        jax.ShapeDtypeStruct((1, ROWS), F32),
    )
    limit = 62 * 1024 * 1024
    outs = pl.pallas_call(
        kernel,
        out_shape=shapes,
        in_specs=[outside] * 8,
        out_specs=(outside,) * 5,
        scratch_shapes=[
            low(HOME, D), low(WORK, D), table, table, table, wide(D), low(ROWS, 480), low(ROWS, 160),
            low(HOME, D), wide(ROWS, 480), wide(ROWS, 160), wide(1, ROWS),
            wide(80, 128),
            low(PACK[0], 128), low(PACK[1], 128),
            low(SIDE, PACK[0], 128), low(SIDE, PACK[1], 128),
            low(D, 384), low(D, 256),
            low(3, GROUP, SIDE * PACK[0]), low(2, GROUP, SIDE * PACK[1]),
            low(3, SIDE * PACK[0], GROUP), low(2, SIDE * PACK[1], GROUP),
            low(D, D),
            low(REACH * SLOT, D), low(REACH * SLOT, D),
            low(WORK, D), wide(WORK, D), low(WORK, D), wide(WORK, 128),
            low(2 * WORK, D), low(D, 2 * WORK),
            wide(D, 384), wide(D, 256),
            low(2, NEAR + 1, GROUP, 384), low(2, NEAR + 1, GROUP, 256),
            low(SIDE, PACK[0], 128), low(SIDE, PACK[1], 128),
            low(SIDE, PACK[0], 128), low(SIDE, PACK[1], 128),
            low(WORK, D), low(REP, 16, D), low(WORK, D), low(REP, 16, D),
            low(WORK, D), low(WORK, D),
            low(REACH * SLOT, D), low(REACH * SLOT, D),
            wide(3, 16, 128), wide(3, SIDE, 16, 128),
            dma((4, SIDE, 2)),
            dma((2, 2, 2, len(STEPS[0]), 2)),
            dma((2, REACH, 2)),
            dma((4, REP, 2)),
            dma((3, SIDE, 2)),
            dma((8,)), dma((5,)),
        ],
        compiler_params=pltpu.CompilerParams(
            collective_id=0, has_side_effects=True, vmem_limit_bytes=limit
        ),
        name="layer",
    )(
        tokens, cotangent, counts.T, hops.T, offsets.T,
        norm_gain, qkv_weight, out_weight,
    )
    outs = pl.pallas_call(
        finish,
        out_shape=shapes,
        in_specs=[outside] * 5,
        out_specs=(outside,) * 5,
        scratch_shapes=[pltpu.VMEM(s.shape, s.dtype) for s in shapes] + [dma((2, 5))],
        compiler_params=pltpu.CompilerParams(vmem_limit_bytes=limit),
        name="finish",
    )(*outs)
    layer_out, input_grad, grad_qkv, grad_out, grad_gain = outs
    return (layer_out, input_grad, grad_qkv, grad_out, grad_gain.reshape(ROWS))


def solution(mesh):
    return jax.shard_map(
        body,
        mesh=mesh,
        in_specs=(P("dp", None), P("dp", None), P(), P(), P(), P(), P("dp", "rep"), P("dp", "rep")),
        out_specs=(P("dp", None), P("dp", None), P("dp", "rep"), P("dp", "rep"), P("dp")),
        check_vma=False,
    )
```

```python
import jax
import jax.numpy as jnp
from jax import lax
from jax.experimental import pallas as pl
from jax.experimental.pallas import tpu as pltpu
from jax.sharding import PartitionSpec as P

MESH = pl.DeviceIdType.MESH
BF16 = jnp.bfloat16
F32 = jnp.float32

D = 1280
HEAD = 80
REACH = 3
SLOT = 16
WORK = 128
HOME = 176
SIDE = 8
REP = 8
ROWS = 20
GROUP = SIDE * ROWS
NEAR = SIDE // 2
IMAGES = 8
EPSILON = 1e-06
NEGATIVE = -1e30
XS = 4
COLS = D // 2

TILES = (3, 2)
FIRST = (0, 384)
PACK = (64, 48)


def dot(a, b, ca=1, cb=0):
    return lax.dot_general(a, b, (((ca,), (cb,)), ((), ())), preferred_element_type=F32)


def onehot(match):
    return jnp.where(match, 1.0, 0.0).astype(BF16)


def iota(shape, dim):
    return lax.broadcasted_iota(jnp.int32, shape, dim)


def div20(v):
    return (v * 3277) >> 16


def images_of(counts, hops, offsets, dev):
    found = []
    start = jnp.int32(0)
    sent = [jnp.int32(0)] * (REACH + 1)
    for j in range(IMAGES):
        count, hop, offset = counts[j, dev], hops[j, dev], offsets[j, dev]
        within = jnp.int32(0)
        for level in range(1, REACH + 1):
            same = hop == level
            within = jnp.where(same, (level - 1) * SLOT + sent[level], within)
            sent[level] = sent[level] + jnp.where(same, count, 0)
        found.append((count, hop, offset, start, within))
        start = start + count
    return found


def spans_index(width, spans):
    lane = iota((1, width), 1)
    index = jnp.full((1, width), -1, jnp.int32)
    for lower, length, source in spans:
        inside = (lane >= lower) & (lane < lower + length)
        index = jnp.where(inside, lane + (source - lower), index)
    return index


FAR = (((80, 48), (128, 32)), ((0, 48), (48, 32)))
PIECES = (FAR[0] + ((0, 80),), FAR[1] + ((80, 80),))


def steps_of(direction):
    return [
        (distance, piece)
        for distance in range(1, NEAR + 1)
        for piece in PIECES[direction]
        if distance < NEAR or piece in FAR[direction]
    ]


STEPS = (steps_of(0), steps_of(1))


def kernel(
    tokens_h, cotangent_h, counts_h, hops_h, offsets_h, gain_h, qkv_h, out_h,
    layer_h, input_h, gq_h, go_h, gg_h,
    tokens, cotangent, counts, hops, offsets, gain_v, qkv_w, out_w,
    input_o, gq_o, go_o, gg_o,
    stage, own0, own1, parts0, parts1, w0, w1, pick0, pick1, put0, put1, perm,
    slots, arrived, work_s, normed_s, hidden_s, inv_s, both_s, both_t,
    g0, g1, ring0, ring1, back0, back1, heard0, heard1,
    hid_p, hid_h, hid_x, hid_r, lay_p, lay_h, lay_x, lay_r, work_g, lay_f, back_slots, back_arr, gain_s, gain_r,
    part_sem, ring_sem, token_sem, x_sem, pair_sem, sum_sem, in_sem, out_sem,
):
    d = lax.axis_index("dp")
    r = lax.axis_index("rep")
    y = d // SIDE
    z = d % SIDE
    x = r // 2
    core = r % 2

    def around(value, step, count):
        return lax.rem(value + (step + count), count)

    def at_y(step):
        return around(y, step, SIDE) * SIDE + z

    def at_z(step):
        return y * SIDE + around(z, step, SIDE)

    def at_dp(step):
        return around(d, step, SIDE * SIDE)

    def at_rep(step):
        return around(r, step, REP)

    def at_x(step):
        return around(x, step, XS) * 2 + core

    other_core = x * 2 + 1 - core

    sent = {}

    def remote(src, dst, sems, dp, rep):
        return pltpu.make_async_remote_copy(
            src_ref=src, dst_ref=dst, send_sem=sems.at[0], recv_sem=sems.at[1],
            device_id=(dp, rep), device_id_type=MESH,
        )

    def send(key, copy):
        copy.start()
        sent[key] = copy

    def got(key):
        sent[key].wait_recv()

    def pair(number, src, dst):
        send(("pair", number), remote(src, dst, pair_sem.at[number], d, other_core))

    barrier = pltpu.get_barrier_semaphore()
    partners = (
        [(at_y(o), r) for o in range(1, SIDE)]
        + [(at_z(o), r) for o in range(1, SIDE)]
        + [(d, at_rep(o)) for o in range(1, REP)]
        + [(at_dp(o), r) for o in (1, 2, 3, -1, -2, -3)]
    )
    for partner in partners:
        pl.semaphore_signal(barrier, inc=1, device_id=partner, device_id_type=MESH)

    loads = [
        pltpu.make_async_copy(src, dst, in_sem.at[i])
        for i, (src, dst) in enumerate(
            (
                (qkv_h, qkv_w), (out_h, out_w), (counts_h, counts), (hops_h, hops),
                (offsets_h, offsets), (tokens_h, tokens), (gain_h, gain_v), (cotangent_h, cotangent),
            )
        )
    ]
    for load in loads:
        load.start()

    stage[...] = jnp.zeros_like(stage)
    for load in loads[0:2]:
        load.wait()
    wide = qkv_w[...].astype(F32)
    wide_out = out_w[...].astype(F32)
    for t in range(3):
        stage[ROWS * t : ROWS * t + ROWS, :] = wide[:, 128 * t : 128 * (t + 1)]
    own0[...] = stage[0 : PACK[0], :].astype(BF16)
    stage[0:ROWS, :] = jnp.concatenate([wide[:, 384:480], wide_out[:, 0:32]], axis=1)
    stage[ROWS : ROWS + ROWS, :] = wide_out[:, 32:160]
    own1[...] = stage[0 : PACK[1], :].astype(BF16)

    pl.semaphore_wait(barrier, len(partners))

    own = (own0, own1)
    parts = (parts0, parts1)
    first_pos = (z, y)
    second_pos = (y, z)
    first_at = (at_z, at_y)
    second_at = (at_y, at_z)
    for o in range(1, SIDE):
        for s in (0, 1):
            send(
                ("part", s, o),
                remote(own[s], parts[s].at[first_pos[s]], part_sem.at[s, o], first_at[s](o), r),
            )
    for load in loads[2:6]:
        load.wait()
    mine = images_of(counts, hops, offsets, d)
    out_index = spans_index(
        REACH * SLOT, [(w, jnp.where(h > 0, c, 0), s) for c, h, o, s, w in mine]
    )
    moved = dot(
        onehot(iota((HOME, REACH * SLOT), 0) == out_index), tokens[...], 0, 0
    ).astype(BF16)
    for half in (0, 1):
        slots[half] = moved[:, COLS * half : COLS * (half + 1)]
    for h in range(1, REACH + 1):
        rows = pl.ds(SLOT * (h - 1), SLOT)
        send(
            ("token", h),
            remote(slots.at[core, rows], arrived.at[core, rows], token_sem.at[0, h - 1], at_dp(h), r),
        )
    for s in (0, 1):
        parts[s][first_pos[s]] = own[s][...]

    picks, puts = (pick0, pick1), (put0, put1)
    for s in (0, 1):
        rows = SIDE * PACK[s]
        lane = iota((1, rows), 1)
        block = lane >> 6 if s == 0 else (lane * 1366) >> 16
        inner = lane - block * PACK[s]
        dense = iota((1, GROUP), 1)
        owner = div20(dense)
        for t in range(TILES[s]):
            row = inner - ROWS * t
            target = jnp.where((row >= 0) & (row < ROWS), block * ROWS + row, -1)
            picks[s][t] = onehot(iota((GROUP, rows), 0) == target)
            source = dense + owner * (PACK[s] - ROWS) + ROWS * t
            puts[s][t] = onehot(iota((rows, GROUP), 0) == source)

    work_spans, work_ids = [], []
    senders = [mine] + [
        images_of(counts, hops, offsets, at_dp(-h)) for h in range(1, REACH + 1)
    ]
    lane = iota((1, WORK), 1)
    ident = jnp.zeros((1, WORK), F32)
    for h, sender in enumerate(senders):
        for j, (c, hop, o, s, w) in enumerate(sender):
            length = jnp.where(hop == h, c, 0)
            work_spans.append((o, length, s if h == 0 else HOME + w))
            inside = (lane >= o) & (lane < o + length)
            ident = jnp.where(inside, float(h * IMAGES + j), ident)
    work_index = spans_index(WORK, work_spans)

    lane = iota((1, D), 1)
    outer = (lane * 6554) >> 20
    inner = lane - outer * GROUP
    middle = div20(inner)
    natural = middle * GROUP + outer * ROWS + (inner - middle * ROWS)
    for b in range(D // 256):
        perm[256 * b : 256 * (b + 1), :] = onehot(iota((256, D), 0) + 256 * b == natural)

    for o in range(1, SIDE):
        for s in (0, 1):
            got(("part", s, o))
    weights = (w0, w1)
    for s in (0, 1):
        block = parts[s][...].reshape(SIDE * PACK[s], 128)
        base = pl.multiple_of(second_pos[s] * GROUP, 16)
        for t in range(TILES[s]):
            weights[s][pl.ds(base, GROUP), 128 * t : 128 * (t + 1)] = dot(
                picks[s][t], block
            ).astype(BF16)

    def gather_copy(s, direction, distance, piece):
        sign = 1 if direction == 0 else -1
        at = around(second_pos[s], -sign * (distance - 1), SIDE)
        rows = pl.ds(pl.multiple_of(at * GROUP + piece[0], 16), piece[1])
        number = STEPS[direction].index((distance, piece))
        return remote(
            weights[s].at[rows], weights[s].at[rows],
            ring_sem.at[0, s, direction, number], second_at[s](sign), r,
        )

    def gather_step(distance):
        for number in range(3 if distance < NEAR else 2):
            for direction in (0, 1):
                piece = PIECES[direction][number]
                for s in (0, 1):
                    if distance > 1:
                        got(("gather", s, direction, distance - 1, piece))
                    send(
                        ("gather", s, direction, distance, piece),
                        gather_copy(s, direction, distance, piece),
                    )

    gather_step(1)

    gather_step(2)
    for h in range(1, REACH + 1):
        got(("token", h))
    pair(0, arrived.at[core], arrived.at[core])
    gather_step(3)

    for load in loads[6:8]:
        load.wait()
    gain = gain_v[...].reshape(1, D)
    got(("pair", 0))
    received = jnp.concatenate([arrived[0], arrived[1]], axis=1)
    work = dot(onehot(iota((HOME, WORK), 0) == work_index), tokens[...], 0, 0) + dot(
        onehot(iota((REACH * SLOT, WORK), 0) + HOME == work_index), received, 0, 0
    )
    work_s[...] = work.astype(BF16)
    centred = work - jnp.mean(work, axis=1, keepdims=True)
    inverse = lax.rsqrt(jnp.mean(centred * centred, axis=1, keepdims=True) + EPSILON)
    normed = centred * inverse
    normed_s[...] = normed
    inv_s[...] = jnp.broadcast_to(inverse, (WORK, 128))
    hidden_s[...] = (normed * gain).astype(BF16)
    gather_step(4)

    both_s[0:WORK, :] = dot(hidden_s[...], perm[...]).astype(BF16)
    both_s[WORK : 2 * WORK, :] = dot(cotangent[...], perm[...]).astype(BF16)
    both_t[...] = both_s[...].astype(F32).T.astype(BF16)
    hidden_t = hidden_s[...].astype(F32).T.astype(BF16)
    ids = jnp.broadcast_to(ident, (WORK, WORK))
    same_image = ids == ids.T
    for direction in (0, 1):
        for distance, piece in STEPS[direction]:
            if (distance + 1, piece) not in STEPS[direction]:
                for s in (0, 1):
                    got(("gather", s, direction, distance, piece))

    pa = dot(hidden_s[...], w0[...]).astype(BF16)
    pb = dot(both_s[...], w1[...]).astype(BF16)
    proj = jnp.concatenate([pa, pb[0:WORK, 0:128]], axis=1)
    scale = HEAD ** (-0.5)
    pieces, attended = [], []
    for j in (0, 1):
        q, k, v = (
            proj[:, 240 * j + HEAD * i : 240 * j + HEAD * (i + 1)] for i in range(3)
        )
        da = pb[WORK : 2 * WORK, 96 + HEAD * j : 96 + HEAD * (j + 1)]
        scores = jnp.where(same_image, dot(q, k, 1, 1) * scale, NEGATIVE)
        exponent = jnp.exp(scores - jnp.max(scores, axis=1, keepdims=True))
        probs = exponent / jnp.sum(exponent, axis=1, keepdims=True)
        probs_low = probs.astype(BF16)
        attended.append(dot(probs_low, v).astype(BF16))
        grad_probs = dot(da, v, 1, 1)
        grad_v = dot(probs_low, da, 0, 0).astype(BF16)
        grad_s = probs * (grad_probs - jnp.sum(probs * grad_probs, axis=1, keepdims=True))
        grad_s = (grad_s * scale).astype(BF16)
        pieces += [
            dot(grad_s, k).astype(BF16),
            dot(grad_s, q, 0, 0).astype(BF16),
            grad_v,
        ]
    mixed = jnp.concatenate(pieces + attended, axis=1)
    mix0 = mixed[:, 0:384]
    mix1 = mixed[:, 384:640]
    in_qkv = iota((WORK, 256), 1) < 96
    mix1_qkv = jnp.where(in_qkv, mix1, jnp.zeros_like(mix1))
    mix1_att = jnp.where(in_qkv, jnp.zeros_like(mix1), mix1)

    g0[...] = dot(hidden_t, mix0)
    g1[...] = dot(both_t[...], jnp.concatenate([mix1_qkv, mix1_att], axis=0))
    totals = (g0, g1)
    rings = (ring0, ring1)

    def sum_copy(s, direction, distance, piece):
        sign = 1 if direction == 0 else -1
        number = STEPS[direction].index((distance, piece))
        rows = pl.ds(*piece)
        return remote(
            rings[s].at[direction, distance, rows], rings[s].at[direction, distance - 1, rows],
            ring_sem.at[1, s, direction, number], second_at[s](sign), r,
        )

    def own_term(s, step, piece):
        at = around(second_pos[s], step, SIDE)
        return totals[s][pl.ds(pl.multiple_of(at * GROUP + piece[0], 16), piece[1]), :]

    def sum_step(distance):
        for number in range(3 if distance < NEAR else 2):
            for direction in (0, 1):
                piece = PIECES[direction][number]
                rows = pl.ds(*piece)
                sign = 1 if direction == 0 else -1
                for s in (0, 1):
                    total = own_term(s, sign * distance, piece)
                    if (distance + 1, piece) in STEPS[direction]:
                        got(("sum", s, direction, distance + 1, piece))
                        total = total + rings[s][direction, distance, rows].astype(F32)
                    rings[s][direction, distance, rows] = total.astype(BF16)
                    send(
                        ("sum", s, direction, distance, piece),
                        sum_copy(s, direction, distance, piece),
                    )

    block = core * XS + x
    my_rows = pl.ds(pl.multiple_of(block * 16, 16), 16)
    my_half = pl.ds(pl.multiple_of(core * 64, 64), 64)
    other_half = pl.ds(pl.multiple_of(64 - core * 64, 64), 64)

    def pair_sum(kind, src, theirs, staged):
        got(("pair", 1 + kind))
        total = src[my_half, :].astype(F32) + theirs[...].astype(F32)
        staged[...] = total.astype(BF16).reshape(XS, 16, D)

    def spread(kind, staged, dst):
        for o in range(1, XS):
            send(
                ("x", kind, o),
                remote(staged.at[around(x, o, XS)], dst.at[x], x_sem.at[kind, o], d, at_x(o)),
            )
        dst[x] = staged[x]

    def summed(kind, dst):
        for o in range(1, XS):
            got(("x", kind, o))
        total = dst[0].astype(F32)
        for i in range(1, XS):
            total = total + dst[i].astype(F32)
        return total

    def share(kind, ref):
        for o in range(1, XS):
            send(
                ("x", kind, o),
                remote(ref.at[my_rows], ref.at[my_rows], x_sem.at[kind, o], d, at_x(o)),
            )

    def share_half(kind, ref):
        for o in range(1, XS):
            got(("x", kind, o))
        pair(1 + kind, ref.at[my_half], ref.at[my_half])

    sum_step(4)
    turned = dot(mix1_qkv, w1[...], 1, 1).astype(BF16)
    hid_p[...] = (dot(mix0, w0[...], 1, 1) + dot(turned, perm[...])).astype(BF16)
    pair(1, hid_p.at[other_half], hid_h)
    turned = dot(mix1_att, w1[...], 1, 1).astype(BF16)
    lay_p[...] = dot(turned, perm[...]).astype(BF16)
    pair(2, lay_p.at[other_half], lay_h)
    pair_sum(0, hid_p, hid_h, hid_x)
    spread(0, hid_x, hid_r)
    sum_step(3)
    pair_sum(1, lay_p, lay_h, lay_x)
    spread(1, lay_x, lay_r)

    back_index = spans_index(
        REACH * SLOT,
        [
            (w, jnp.where(hop == h, c, 0), o)
            for h in range(1, REACH + 1)
            for c, hop, o, s, w in senders[h]
        ],
    )
    home_index = spans_index(
        HOME, [(s, c, jnp.where(h == 0, o, WORK + w)) for c, h, o, s, w in mine]
    )

    grad_hidden = summed(0, hid_r)
    norm_rows = normed_s[my_rows, :]
    grad_normed = grad_hidden * gain
    correction = (
        grad_normed
        - jnp.mean(grad_normed, axis=1, keepdims=True)
        - norm_rows * jnp.mean(grad_normed * norm_rows, axis=1, keepdims=True)
    )
    work_g[my_rows, :] = (
        cotangent[my_rows, :].astype(F32) + inv_s[my_rows, 0:1] * correction
    ).astype(BF16)
    share(2, work_g)
    row_gain = jnp.sum(grad_hidden * norm_rows, axis=0, keepdims=True)
    gain_s[...] = jnp.zeros_like(gain_s)
    for t in range(D // 128):
        gain_s[0, t : t + 1, :] = row_gain[:, 128 * t : 128 * (t + 1)]

    gain_at = (
        (r, lambda o: (d, at_rep(o))),
        (y, lambda o: (at_y(o), r)),
        (z, lambda o: (at_z(o), r)),
    )

    def send_gain(level):
        me, peer = gain_at[level]
        for o in range(1, SIDE):
            send(
                ("gain", level, o),
                remote(gain_s.at[level], gain_r.at[level, me], sum_sem.at[level, o], *peer(o)),
            )
        gain_r[level, me] = gain_s[level]

    def sum_gain(level):
        for o in range(1, SIDE):
            got(("gain", level, o))
        total = gain_r[level, 0]
        for i in range(1, SIDE):
            total = total + gain_r[level, i]
        return total

    send_gain(0)

    sum_step(2)
    share_half(2, work_g)
    projected = summed(1, lay_r)
    lay_f[my_rows, :] = (work_s[my_rows, :].astype(F32) + projected).astype(BF16)
    share(3, lay_f)
    got(("pair", 3))
    moved = dot(
        onehot(iota((WORK, REACH * SLOT), 0) == back_index), work_g[...], 0, 0
    ).astype(BF16)
    for half in (0, 1):
        back_slots[half] = moved[:, COLS * half : COLS * (half + 1)]
    for h in range(1, REACH + 1):
        rows = pl.ds(SLOT * (h - 1), SLOT)
        send(
            ("back", h),
            remote(back_slots.at[core, rows], back_arr.at[core, rows], token_sem.at[1, h - 1], at_dp(-h), r),
        )
    gain_s[1] = sum_gain(0)
    send_gain(1)

    sum_step(1)
    share_half(3, lay_f)
    for h in range(1, REACH + 1):
        got(("back", h))
    pair(5, back_arr.at[core], back_arr.at[core])
    gain_s[2] = sum_gain(1)
    send_gain(2)

    backs, heards = (back0, back1), (heard0, heard1)
    for s in (0, 1):
        for direction in (0, 1):
            for piece in PIECES[direction]:
                got(("sum", s, direction, 1, piece))
        total = own_term(s, 0, (0, GROUP))
        for direction in (0, 1):
            total = total + rings[s][direction, 0].astype(F32)
        dense = total.astype(BF16)
        spreadout = dot(puts[s][0], dense[:, 0:128])
        for t in range(1, TILES[s]):
            spreadout = spreadout + dot(puts[s][t], dense[:, 128 * t : 128 * (t + 1)])
        backs[s][...] = spreadout.astype(BF16).reshape(SIDE, PACK[s], 128)
        for o in range(1, SIDE):
            to = around(first_pos[s], o, SIDE)
            send(
                ("last", s, o),
                remote(backs[s].at[to], heards[s].at[first_pos[s]], part_sem.at[2 + s, o], first_at[s](o), r),
            )
        heards[s][first_pos[s]] = backs[s][first_pos[s]]

    stores = []

    def store(src, dst):
        copy = pltpu.make_async_copy(src, dst, out_sem.at[len(stores)])
        copy.start()
        stores.append(copy)

    got(("pair", 5))
    received = jnp.concatenate([back_arr[0], back_arr[1]], axis=1)
    input_o[...] = (
        dot(onehot(iota((WORK, HOME), 0) == home_index), work_g[...], 0, 0)
        + dot(onehot(iota((REACH * SLOT, HOME), 0) + WORK == home_index), received, 0, 0)
    ).astype(BF16)
    store(input_o, input_h)
    got(("pair", 4))
    store(lay_f, layer_h)

    tiles = []
    for s in (0, 1):
        for o in range(1, SIDE):
            got(("last", s, o))
        total = heards[s][0].astype(F32)
        for i in range(1, SIDE):
            total = total + heards[s][i].astype(F32)
        tiles += [total[ROWS * t : ROWS * t + ROWS, :] for t in range(TILES[s])]
    grad_qkv = jnp.concatenate(tiles[0:3] + [tiles[3][:, 0:96]], axis=1)
    gq_o[...] = grad_qkv
    go_o[...] = jnp.concatenate([tiles[3][:, 96:128], tiles[4]], axis=1)
    store(gq_o, gq_h)
    store(go_o, go_h)

    total = sum_gain(2)
    row = jnp.concatenate([total[t : t + 1, :] for t in range(D // 128)], axis=1)
    row = pltpu.roll(jnp.broadcast_to(row, (8, D)), lax.rem(D - ROWS * d, D), 1)
    gg_o[...] = row[0:1, 0:ROWS]
    store(gg_o, gg_h)

    for copy in stores:
        copy.wait()
    for copy in sent.values():
        copy.wait_send()


def finish(*refs):
    held, outs, rooms, sems = refs[0:5], refs[5:10], refs[10:15], refs[15]
    loads = [pltpu.make_async_copy(h, v, sems.at[0, i]) for i, (h, v) in enumerate(zip(held, rooms))]
    stores = [pltpu.make_async_copy(v, o, sems.at[1, i]) for i, (v, o) in enumerate(zip(rooms, outs))]
    for load in loads:
        load.start()
    for load, store in zip(loads, stores):
        load.wait()
        store.start()
    for store in stores:
        store.wait()


def body(tokens, cotangent, counts, hops, offsets, norm_gain, qkv_weight, out_weight):
    outside = pl.BlockSpec(memory_space=pl.ANY)
    dma = pltpu.SemaphoreType.DMA
    low = lambda *shape: pltpu.VMEM(shape, BF16)
    wide = lambda *shape: pltpu.VMEM(shape, F32)
    table = pltpu.SMEM((IMAGES, SIDE * SIDE), jnp.int32)
    shapes = (
        jax.ShapeDtypeStruct((WORK, D), BF16),
        jax.ShapeDtypeStruct((HOME, D), BF16),
        jax.ShapeDtypeStruct((ROWS, 480), F32),
        jax.ShapeDtypeStruct((ROWS, 160), F32),
        jax.ShapeDtypeStruct((1, ROWS), F32),
    )
    limit = 62 * 1024 * 1024
    outs = pl.pallas_call(
        kernel,
        out_shape=shapes,
        in_specs=[outside] * 8,
        out_specs=(outside,) * 5,
        scratch_shapes=[
            low(HOME, D), low(WORK, D), table, table, table, wide(D), low(ROWS, 480), low(ROWS, 160),
            low(HOME, D), wide(ROWS, 480), wide(ROWS, 160), wide(1, ROWS),
            wide(64, 128),
            low(PACK[0], 128), low(PACK[1], 128),
            low(SIDE, PACK[0], 128), low(SIDE, PACK[1], 128),
            low(D, 384), low(D, 256),
            low(3, GROUP, SIDE * PACK[0]), low(2, GROUP, SIDE * PACK[1]),
            low(3, SIDE * PACK[0], GROUP), low(2, SIDE * PACK[1], GROUP),
            low(D, D),
            low(2, REACH * SLOT, COLS), low(2, REACH * SLOT, COLS),
            low(WORK, D), wide(WORK, D), low(WORK, D), wide(WORK, 128),
            low(2 * WORK, D), low(D, 2 * WORK),
            wide(D, 384), wide(D, 256),
            low(2, NEAR + 1, GROUP, 384), low(2, NEAR + 1, GROUP, 256),
            low(SIDE, PACK[0], 128), low(SIDE, PACK[1], 128),
            low(SIDE, PACK[0], 128), low(SIDE, PACK[1], 128),
            low(WORK, D), low(64, D), low(XS, 16, D), low(XS, 16, D),
            low(WORK, D), low(64, D), low(XS, 16, D), low(XS, 16, D),
            low(WORK, D), low(WORK, D),
            low(2, REACH * SLOT, COLS), low(2, REACH * SLOT, COLS),
            wide(3, 16, 128), wide(3, SIDE, 16, 128),
            dma((4, SIDE, 2)),
            dma((2, 2, 2, len(STEPS[0]), 2)),
            dma((2, REACH, 2)),
            dma((4, XS, 2)), dma((6, 2)),
            dma((3, SIDE, 2)),
            dma((8,)), dma((5,)),
        ],
        compiler_params=pltpu.CompilerParams(
            collective_id=0, has_side_effects=True, vmem_limit_bytes=limit
        ),
        name="layer",
    )(
        tokens, cotangent, counts.T, hops.T, offsets.T,
        norm_gain, qkv_weight, out_weight,
    )
    outs = pl.pallas_call(
        finish,
        out_shape=shapes,
        in_specs=[outside] * 5,
        out_specs=(outside,) * 5,
        scratch_shapes=[pltpu.VMEM(s.shape, s.dtype) for s in shapes] + [dma((2, 5))],
        compiler_params=pltpu.CompilerParams(vmem_limit_bytes=limit),
        name="finish",
    )(*outs)
    layer_out, input_grad, grad_qkv, grad_out, grad_gain = outs
    return (layer_out, input_grad, grad_qkv, grad_out, grad_gain.reshape(ROWS))


def solution(mesh):
    return jax.shard_map(
        body,
        mesh=mesh,
        in_specs=(P("dp", None), P("dp", None), P(), P(), P(), P(), P("dp", "rep"), P("dp", "rep")),
        out_specs=(P("dp", None), P("dp", None), P("dp", "rep"), P("dp", "rep"), P("dp")),
        check_vma=False,
    )
```

```python
import jax
import jax.numpy as jnp
from jax import lax
from jax.experimental import pallas as pl
from jax.experimental.pallas import tpu as pltpu
from jax.sharding import PartitionSpec as P

MESH = pl.DeviceIdType.MESH
BF16 = jnp.bfloat16
F32 = jnp.float32

D = 1280
HEAD = 80
REACH = 3
SLOT = 16
WORK = 128
HOME = 176
SIDE = 8
REP = 8
ROWS = 20
GROUP = SIDE * ROWS
NEAR = SIDE // 2
IMAGES = 8
EPSILON = 1e-06
NEGATIVE = -1e30
XS = 4
COLS = D // 2

TILES = (3, 2)
FIRST = (0, 384)
PACK = (64, 48)


def dot(a, b, ca=1, cb=0):
    return lax.dot_general(a, b, (((ca,), (cb,)), ((), ())), preferred_element_type=F32)


def onehot(match):
    return jnp.where(match, 1.0, 0.0).astype(BF16)


def iota(shape, dim):
    return lax.broadcasted_iota(jnp.int32, shape, dim)


def div20(v):
    return (v * 3277) >> 16


def images_of(counts, hops, offsets, dev):
    found = []
    start = jnp.int32(0)
    sent = [jnp.int32(0)] * (REACH + 1)
    for j in range(IMAGES):
        count, hop, offset = counts[j, dev], hops[j, dev], offsets[j, dev]
        within = jnp.int32(0)
        for level in range(1, REACH + 1):
            same = hop == level
            within = jnp.where(same, (level - 1) * SLOT + sent[level], within)
            sent[level] = sent[level] + jnp.where(same, count, 0)
        found.append((count, hop, offset, start, within))
        start = start + count
    return found


def spans_index(width, spans):
    lane = iota((1, width), 1)
    index = jnp.full((1, width), -1, jnp.int32)
    for lower, length, source in spans:
        inside = (lane >= lower) & (lane < lower + length)
        index = jnp.where(inside, lane + (source - lower), index)
    return index


FAR = (((80, 48), (128, 32)), ((0, 48), (48, 32)))
PIECES = (FAR[0] + ((0, 80),), FAR[1] + ((80, 80),))


def steps_of(direction):
    return [
        (distance, piece)
        for distance in range(1, NEAR + 1)
        for piece in PIECES[direction]
        if distance < NEAR or piece in FAR[direction]
    ]


STEPS = (steps_of(0), steps_of(1))


def kernel(
    tokens_h, cotangent_h, counts_h, hops_h, offsets_h, gain_h, qkv_h, out_h,
    layer_h, input_h, gq_h, go_h, gg_h,
    tokens, cotangent, counts, hops, offsets, gain_v, qkv_w, out_w,
    input_o, gq_o, go_o, gg_o,
    stage, own0, own1, parts0, parts1, w0, w1, pick0, pick1, put0, put1, perm,
    slots, arrived, work_s, normed_s, hidden_s, inv_s, both_s, both_t,
    g0, g1, ring0, ring1, back0, back1, heard0, heard1,
    hid_p, hid_h, hid_x, hid_r, lay_p, lay_h, lay_x, lay_r, work_g, lay_f, back_slots, back_arr, gain_s, gain_r,
    part_sem, ring_sem, token_sem, x_sem, pair_sem, sum_sem, in_sem, out_sem,
):
    d = lax.axis_index("dp")
    r = lax.axis_index("rep")
    y = d // SIDE
    z = d % SIDE
    x = r // 2
    core = r % 2

    def around(value, step, count):
        return lax.rem(value + (step + count), count)

    def at_y(step):
        return around(y, step, SIDE) * SIDE + z

    def at_z(step):
        return y * SIDE + around(z, step, SIDE)

    def at_dp(step):
        return around(d, step, SIDE * SIDE)

    def at_rep(step):
        return around(r, step, REP)

    def at_x(step):
        return around(x, step, XS) * 2 + core

    other_core = x * 2 + 1 - core
    block = core * XS + x
    my_rows = pl.ds(pl.multiple_of(block * 16, 16), 16)
    my_half = pl.ds(pl.multiple_of(core * 64, 64), 64)
    other_half = pl.ds(pl.multiple_of(64 - core * 64, 64), 64)

    sent = {}

    def remote(src, dst, sems, dp, rep):
        return pltpu.make_async_remote_copy(
            src_ref=src, dst_ref=dst, send_sem=sems.at[0], recv_sem=sems.at[1],
            device_id=(dp, rep), device_id_type=MESH,
        )

    def send(key, copy):
        copy.start()
        sent[key] = copy

    def got(key):
        sent[key].wait_recv()

    def pair(number, src, dst):
        send(("pair", number), remote(src, dst, pair_sem.at[number], d, other_core))

    barrier = pltpu.get_barrier_semaphore()
    partners = (
        [(at_y(o), r) for o in range(1, SIDE)]
        + [(at_z(o), r) for o in range(1, SIDE)]
        + [(d, at_rep(o)) for o in range(1, REP)]
        + [(at_dp(o), r) for o in (1, 2, 3, -1, -2, -3)]
    )
    for partner in partners:
        pl.semaphore_signal(barrier, inc=1, device_id=partner, device_id_type=MESH)

    loads = [
        pltpu.make_async_copy(src, dst, in_sem.at[i])
        for i, (src, dst) in enumerate(
            (
                (qkv_h, qkv_w), (out_h, out_w), (counts_h, counts), (hops_h, hops),
                (offsets_h, offsets), (tokens_h, tokens), (gain_h, gain_v), (cotangent_h, cotangent),
            )
        )
    ]
    for load in loads:
        load.start()

    stage[...] = jnp.zeros_like(stage)
    for load in loads[0:2]:
        load.wait()
    wide = qkv_w[...].astype(F32)
    wide_out = out_w[...].astype(F32)
    for t in range(3):
        stage[ROWS * t : ROWS * t + ROWS, :] = wide[:, 128 * t : 128 * (t + 1)]
    own0[...] = stage[0 : PACK[0], :].astype(BF16)
    stage[0:ROWS, :] = jnp.concatenate([wide[:, 384:480], wide_out[:, 0:32]], axis=1)
    stage[ROWS : ROWS + ROWS, :] = wide_out[:, 32:160]
    own1[...] = stage[0 : PACK[1], :].astype(BF16)

    pl.semaphore_wait(barrier, len(partners))

    own = (own0, own1)
    parts = (parts0, parts1)
    first_pos = (z, y)
    second_pos = (y, z)
    first_at = (at_z, at_y)
    second_at = (at_y, at_z)
    for o in range(1, SIDE):
        for s in (0, 1):
            send(
                ("part", s, o),
                remote(own[s], parts[s].at[first_pos[s]], part_sem.at[s, o], first_at[s](o), r),
            )
    for load in loads[2:6]:
        load.wait()
    mine = images_of(counts, hops, offsets, d)
    out_index = spans_index(
        REACH * SLOT, [(w, jnp.where(h > 0, c, 0), s) for c, h, o, s, w in mine]
    )
    moved = dot(
        onehot(iota((HOME, REACH * SLOT), 0) == out_index), tokens[...], 0, 0
    ).astype(BF16)
    for half in (0, 1):
        slots[half] = moved[:, COLS * half : COLS * (half + 1)]
    for h in range(1, REACH + 1):
        rows = pl.ds(SLOT * (h - 1), SLOT)
        send(
            ("token", h),
            remote(slots.at[core, rows], arrived.at[core, rows], token_sem.at[0, h - 1], at_dp(h), r),
        )
    for s in (0, 1):
        parts[s][first_pos[s]] = own[s][...]

    picks, puts = (pick0, pick1), (put0, put1)
    for s in (0, 1):
        rows = SIDE * PACK[s]
        lane = iota((1, rows), 1)
        block = lane >> 6 if s == 0 else (lane * 1366) >> 16
        inner = lane - block * PACK[s]
        dense = iota((1, GROUP), 1)
        owner = div20(dense)
        for t in range(TILES[s]):
            row = inner - ROWS * t
            target = jnp.where((row >= 0) & (row < ROWS), block * ROWS + row, -1)
            picks[s][t] = onehot(iota((GROUP, rows), 0) == target)
            source = dense + owner * (PACK[s] - ROWS) + ROWS * t
            puts[s][t] = onehot(iota((rows, GROUP), 0) == source)

    work_spans, work_ids = [], []
    senders = [mine] + [
        images_of(counts, hops, offsets, at_dp(-h)) for h in range(1, REACH + 1)
    ]
    lane = iota((1, WORK), 1)
    ident = jnp.zeros((1, WORK), F32)
    for h, sender in enumerate(senders):
        for j, (c, hop, o, s, w) in enumerate(sender):
            length = jnp.where(hop == h, c, 0)
            work_spans.append((o, length, s if h == 0 else HOME + w))
            inside = (lane >= o) & (lane < o + length)
            ident = jnp.where(inside, float(h * IMAGES + j), ident)
    work_index = spans_index(WORK, work_spans)

    lane = iota((1, D), 1)
    outer = (lane * 6554) >> 20
    inner = lane - outer * GROUP
    middle = div20(inner)
    natural = middle * GROUP + outer * ROWS + (inner - middle * ROWS)
    for b in range(D // 256):
        perm[256 * b : 256 * (b + 1), :] = onehot(iota((256, D), 0) + 256 * b == natural)

    for o in range(1, SIDE):
        for s in (0, 1):
            got(("part", s, o))
    weights = (w0, w1)
    for s in (0, 1):
        block = parts[s][...].reshape(SIDE * PACK[s], 128)
        base = pl.multiple_of(second_pos[s] * GROUP, 16)
        for t in range(TILES[s]):
            weights[s][pl.ds(base, GROUP), 128 * t : 128 * (t + 1)] = dot(
                picks[s][t], block
            ).astype(BF16)

    def gather_copy(s, direction, distance, piece):
        sign = 1 if direction == 0 else -1
        at = around(second_pos[s], -sign * (distance - 1), SIDE)
        rows = pl.ds(pl.multiple_of(at * GROUP + piece[0], 16), piece[1])
        number = STEPS[direction].index((distance, piece))
        return remote(
            weights[s].at[rows], weights[s].at[rows],
            ring_sem.at[0, s, direction, number], second_at[s](sign), r,
        )

    def gather_step(distance):
        for number in range(3 if distance < NEAR else 2):
            for direction in (0, 1):
                piece = PIECES[direction][number]
                for s in (0, 1):
                    if distance > 1:
                        got(("gather", s, direction, distance - 1, piece))
                    send(
                        ("gather", s, direction, distance, piece),
                        gather_copy(s, direction, distance, piece),
                    )

    gather_step(1)

    gather_step(2)
    for h in range(1, REACH + 1):
        got(("token", h))
    pair(0, arrived.at[core], arrived.at[core])
    gather_step(3)

    for load in loads[6:8]:
        load.wait()
    gain = gain_v[...].reshape(1, D)
    got(("pair", 0))
    received = jnp.concatenate([arrived[0], arrived[1]], axis=1)
    work = dot(onehot(iota((HOME, WORK), 0) == work_index), tokens[...], 0, 0) + dot(
        onehot(iota((REACH * SLOT, WORK), 0) + HOME == work_index), received, 0, 0
    )
    work_s[...] = work.astype(BF16)
    centred = work - jnp.mean(work, axis=1, keepdims=True)
    inverse = lax.rsqrt(jnp.mean(centred * centred, axis=1, keepdims=True) + EPSILON)
    normed = centred * inverse
    normed_s[...] = normed
    inv_s[...] = jnp.broadcast_to(inverse, (WORK, 128))
    hidden_s[...] = (normed * gain).astype(BF16)
    gather_step(4)

    both_s[0:WORK, :] = dot(hidden_s[...], perm[...]).astype(BF16)
    both_s[WORK : 2 * WORK, :] = dot(cotangent[...], perm[...]).astype(BF16)
    both_t[...] = both_s[...].astype(F32).T.astype(BF16)
    hidden_t = hidden_s[...].astype(F32).T.astype(BF16)
    ids = jnp.broadcast_to(ident, (WORK, WORK))
    same_image = ids == ids.T
    for direction in (0, 1):
        for distance, piece in STEPS[direction]:
            if (distance + 1, piece) not in STEPS[direction]:
                for s in (0, 1):
                    got(("gather", s, direction, distance, piece))

    pa = dot(hidden_s[...], w0[...]).astype(BF16)
    pb = dot(both_s[...], w1[...]).astype(BF16)
    proj = jnp.concatenate([pa, pb[0:WORK, 0:128]], axis=1)
    scale = HEAD ** (-0.5)
    pieces, attended = [], []
    for j in (0, 1):
        q, k, v = (
            proj[:, 240 * j + HEAD * i : 240 * j + HEAD * (i + 1)] for i in range(3)
        )
        da = pb[WORK : 2 * WORK, 96 + HEAD * j : 96 + HEAD * (j + 1)]
        scores = jnp.where(same_image, dot(q, k, 1, 1) * scale, NEGATIVE)
        exponent = jnp.exp(scores - jnp.max(scores, axis=1, keepdims=True))
        probs = exponent / jnp.sum(exponent, axis=1, keepdims=True)
        probs_low = probs.astype(BF16)
        attended.append(dot(probs_low, v).astype(BF16))
        grad_probs = dot(da, v, 1, 1)
        grad_v = dot(probs_low, da, 0, 0).astype(BF16)
        grad_s = probs * (grad_probs - jnp.sum(probs * grad_probs, axis=1, keepdims=True))
        grad_s = (grad_s * scale).astype(BF16)
        pieces += [
            dot(grad_s, k).astype(BF16),
            dot(grad_s, q, 0, 0).astype(BF16),
            grad_v,
        ]
    mixed = jnp.concatenate(pieces + attended, axis=1)
    mix0 = mixed[:, 0:384]
    mix1 = mixed[:, 384:640]
    in_qkv = iota((WORK, 256), 1) < 96
    mix1_qkv = jnp.where(in_qkv, mix1, jnp.zeros_like(mix1))
    mix1_att = jnp.where(in_qkv, jnp.zeros_like(mix1), mix1)

    turned = dot(mix1_qkv, w1[...], 1, 1).astype(BF16)
    hid_p[...] = (dot(mix0, w0[...], 1, 1) + dot(turned, perm[...])).astype(BF16)
    pair(1, hid_p.at[other_half], hid_h)

    g0[...] = dot(hidden_t, mix0)
    g1[...] = dot(both_t[...], jnp.concatenate([mix1_qkv, mix1_att], axis=0))
    totals = (g0, g1)
    rings = (ring0, ring1)

    def sum_copy(s, direction, distance, piece):
        sign = 1 if direction == 0 else -1
        number = STEPS[direction].index((distance, piece))
        rows = pl.ds(*piece)
        return remote(
            rings[s].at[direction, distance, rows], rings[s].at[direction, distance - 1, rows],
            ring_sem.at[1, s, direction, number], second_at[s](sign), r,
        )

    def own_term(s, step, piece):
        at = around(second_pos[s], step, SIDE)
        return totals[s][pl.ds(pl.multiple_of(at * GROUP + piece[0], 16), piece[1]), :]

    def sum_step(distance):
        for number in range(3 if distance < NEAR else 2):
            for direction in (0, 1):
                piece = PIECES[direction][number]
                rows = pl.ds(*piece)
                sign = 1 if direction == 0 else -1
                for s in (0, 1):
                    total = own_term(s, sign * distance, piece)
                    if (distance + 1, piece) in STEPS[direction]:
                        got(("sum", s, direction, distance + 1, piece))
                        total = total + rings[s][direction, distance, rows].astype(F32)
                    rings[s][direction, distance, rows] = total.astype(BF16)
                    send(
                        ("sum", s, direction, distance, piece),
                        sum_copy(s, direction, distance, piece),
                    )

    def pair_sum(kind, src, theirs, staged):
        got(("pair", 1 + kind))
        total = src[my_half, :].astype(F32) + theirs[...].astype(F32)
        staged[...] = total.astype(BF16).reshape(XS, 16, D)

    def spread(kind, staged, dst):
        for o in range(1, XS):
            send(
                ("x", kind, o),
                remote(staged.at[around(x, o, XS)], dst.at[x], x_sem.at[kind, o], d, at_x(o)),
            )
        dst[x] = staged[x]

    def summed(kind, dst):
        for o in range(1, XS):
            got(("x", kind, o))
        total = dst[0].astype(F32)
        for i in range(1, XS):
            total = total + dst[i].astype(F32)
        return total

    def share(kind, ref):
        for o in range(1, XS):
            send(
                ("x", kind, o),
                remote(ref.at[my_rows], ref.at[my_rows], x_sem.at[kind, o], d, at_x(o)),
            )

    def share_half(kind, ref):
        for o in range(1, XS):
            got(("x", kind, o))
        pair(1 + kind, ref.at[my_half], ref.at[my_half])

    sum_step(4)
    pair_sum(0, hid_p, hid_h, hid_x)
    spread(0, hid_x, hid_r)
    turned = dot(mix1_att, w1[...], 1, 1).astype(BF16)
    lay_p[...] = dot(turned, perm[...]).astype(BF16)
    pair(2, lay_p.at[other_half], lay_h)
    sum_step(3)
    pair_sum(1, lay_p, lay_h, lay_x)
    spread(1, lay_x, lay_r)

    back_index = spans_index(
        REACH * SLOT,
        [
            (w, jnp.where(hop == h, c, 0), o)
            for h in range(1, REACH + 1)
            for c, hop, o, s, w in senders[h]
        ],
    )
    home_index = spans_index(
        HOME, [(s, c, jnp.where(h == 0, o, WORK + w)) for c, h, o, s, w in mine]
    )

    grad_hidden = summed(0, hid_r)
    norm_rows = normed_s[my_rows, :]
    grad_normed = grad_hidden * gain
    correction = (
        grad_normed
        - jnp.mean(grad_normed, axis=1, keepdims=True)
        - norm_rows * jnp.mean(grad_normed * norm_rows, axis=1, keepdims=True)
    )
    work_g[my_rows, :] = (
        cotangent[my_rows, :].astype(F32) + inv_s[my_rows, 0:1] * correction
    ).astype(BF16)
    share(2, work_g)
    row_gain = jnp.sum(grad_hidden * norm_rows, axis=0, keepdims=True)
    gain_s[...] = jnp.zeros_like(gain_s)
    for t in range(D // 128):
        gain_s[0, t : t + 1, :] = row_gain[:, 128 * t : 128 * (t + 1)]

    gain_at = (
        (r, lambda o: (d, at_rep(o))),
        (y, lambda o: (at_y(o), r)),
        (z, lambda o: (at_z(o), r)),
    )

    def send_gain(level):
        me, peer = gain_at[level]
        for o in range(1, SIDE):
            send(
                ("gain", level, o),
                remote(gain_s.at[level], gain_r.at[level, me], sum_sem.at[level, o], *peer(o)),
            )
        gain_r[level, me] = gain_s[level]

    def sum_gain(level):
        for o in range(1, SIDE):
            got(("gain", level, o))
        total = gain_r[level, 0]
        for i in range(1, SIDE):
            total = total + gain_r[level, i]
        return total

    send_gain(0)

    sum_step(2)
    projected = summed(1, lay_r)
    lay_f[my_rows, :] = (work_s[my_rows, :].astype(F32) + projected).astype(BF16)
    share(3, lay_f)
    sum_step(1)
    share_half(2, work_g)
    gain_s[1] = sum_gain(0)
    send_gain(1)
    got(("pair", 3))
    moved = dot(
        onehot(iota((WORK, REACH * SLOT), 0) == back_index), work_g[...], 0, 0
    ).astype(BF16)
    for half in (0, 1):
        back_slots[half] = moved[:, COLS * half : COLS * (half + 1)]
    for h in range(1, REACH + 1):
        rows = pl.ds(SLOT * (h - 1), SLOT)
        send(
            ("back", h),
            remote(back_slots.at[core, rows], back_arr.at[core, rows], token_sem.at[1, h - 1], at_dp(-h), r),
        )

    backs, heards = (back0, back1), (heard0, heard1)
    for s in (0, 1):
        for direction in (0, 1):
            for piece in PIECES[direction]:
                got(("sum", s, direction, 1, piece))
        total = own_term(s, 0, (0, GROUP))
        for direction in (0, 1):
            total = total + rings[s][direction, 0].astype(F32)
        dense = total.astype(BF16)
        spreadout = dot(puts[s][0], dense[:, 0:128])
        for t in range(1, TILES[s]):
            spreadout = spreadout + dot(puts[s][t], dense[:, 128 * t : 128 * (t + 1)])
        backs[s][...] = spreadout.astype(BF16).reshape(SIDE, PACK[s], 128)
        for o in range(1, SIDE):
            to = around(first_pos[s], o, SIDE)
            send(
                ("last", s, o),
                remote(backs[s].at[to], heards[s].at[first_pos[s]], part_sem.at[2 + s, o], first_at[s](o), r),
            )
        heards[s][first_pos[s]] = backs[s][first_pos[s]]

    share_half(3, lay_f)
    gain_s[2] = sum_gain(1)
    send_gain(2)
    stores = []

    def store(src, dst):
        copy = pltpu.make_async_copy(src, dst, out_sem.at[len(stores)])
        copy.start()
        stores.append(copy)

    for h in range(1, REACH + 1):
        got(("back", h))
    pair(5, back_arr.at[core], back_arr.at[core])
    got(("pair", 5))
    received = jnp.concatenate([back_arr[0], back_arr[1]], axis=1)
    input_o[...] = (
        dot(onehot(iota((WORK, HOME), 0) == home_index), work_g[...], 0, 0)
        + dot(onehot(iota((REACH * SLOT, HOME), 0) + WORK == home_index), received, 0, 0)
    ).astype(BF16)
    store(input_o, input_h)
    got(("pair", 4))
    store(lay_f, layer_h)

    tiles = []
    for s in (0, 1):
        for o in range(1, SIDE):
            got(("last", s, o))
        total = heards[s][0].astype(F32)
        for i in range(1, SIDE):
            total = total + heards[s][i].astype(F32)
        tiles += [total[ROWS * t : ROWS * t + ROWS, :] for t in range(TILES[s])]
    grad_qkv = jnp.concatenate(tiles[0:3] + [tiles[3][:, 0:96]], axis=1)
    gq_o[...] = grad_qkv
    go_o[...] = jnp.concatenate([tiles[3][:, 96:128], tiles[4]], axis=1)
    store(gq_o, gq_h)
    store(go_o, go_h)

    total = sum_gain(2)
    row = jnp.concatenate([total[t : t + 1, :] for t in range(D // 128)], axis=1)
    row = pltpu.roll(jnp.broadcast_to(row, (8, D)), lax.rem(D - ROWS * d, D), 1)
    gg_o[...] = row[0:1, 0:ROWS]
    store(gg_o, gg_h)

    for copy in stores:
        copy.wait()
    for copy in sent.values():
        copy.wait_send()


def finish(*refs):
    held, outs, rooms, sems = refs[0:5], refs[5:10], refs[10:15], refs[15]
    loads = [pltpu.make_async_copy(h, v, sems.at[0, i]) for i, (h, v) in enumerate(zip(held, rooms))]
    stores = [pltpu.make_async_copy(v, o, sems.at[1, i]) for i, (v, o) in enumerate(zip(rooms, outs))]
    for load in loads:
        load.start()
    for load, store in zip(loads, stores):
        load.wait()
        store.start()
    for store in stores:
        store.wait()


def body(tokens, cotangent, counts, hops, offsets, norm_gain, qkv_weight, out_weight):
    outside = pl.BlockSpec(memory_space=pl.ANY)
    dma = pltpu.SemaphoreType.DMA
    low = lambda *shape: pltpu.VMEM(shape, BF16)
    wide = lambda *shape: pltpu.VMEM(shape, F32)
    table = pltpu.SMEM((IMAGES, SIDE * SIDE), jnp.int32)
    shapes = (
        jax.ShapeDtypeStruct((WORK, D), BF16),
        jax.ShapeDtypeStruct((HOME, D), BF16),
        jax.ShapeDtypeStruct((ROWS, 480), F32),
        jax.ShapeDtypeStruct((ROWS, 160), F32),
        jax.ShapeDtypeStruct((1, ROWS), F32),
    )
    limit = 62 * 1024 * 1024
    outs = pl.pallas_call(
        kernel,
        out_shape=shapes,
        in_specs=[outside] * 8,
        out_specs=(outside,) * 5,
        scratch_shapes=[
            low(HOME, D), low(WORK, D), table, table, table, wide(D), low(ROWS, 480), low(ROWS, 160),
            low(HOME, D), wide(ROWS, 480), wide(ROWS, 160), wide(1, ROWS),
            wide(64, 128),
            low(PACK[0], 128), low(PACK[1], 128),
            low(SIDE, PACK[0], 128), low(SIDE, PACK[1], 128),
            low(D, 384), low(D, 256),
            low(3, GROUP, SIDE * PACK[0]), low(2, GROUP, SIDE * PACK[1]),
            low(3, SIDE * PACK[0], GROUP), low(2, SIDE * PACK[1], GROUP),
            low(D, D),
            low(2, REACH * SLOT, COLS), low(2, REACH * SLOT, COLS),
            low(WORK, D), wide(WORK, D), low(WORK, D), wide(WORK, 128),
            low(2 * WORK, D), low(D, 2 * WORK),
            wide(D, 384), wide(D, 256),
            low(2, NEAR + 1, GROUP, 384), low(2, NEAR + 1, GROUP, 256),
            low(SIDE, PACK[0], 128), low(SIDE, PACK[1], 128),
            low(SIDE, PACK[0], 128), low(SIDE, PACK[1], 128),
            low(WORK, D), low(64, D), low(XS, 16, D), low(XS, 16, D),
            low(WORK, D), low(64, D), low(XS, 16, D), low(XS, 16, D),
            low(WORK, D), low(WORK, D),
            low(2, REACH * SLOT, COLS), low(2, REACH * SLOT, COLS),
            wide(3, 16, 128), wide(3, SIDE, 16, 128),
            dma((4, SIDE, 2)),
            dma((2, 2, 2, len(STEPS[0]), 2)),
            dma((2, REACH, 2)),
            dma((4, XS, 2)), dma((6, 2)),
            dma((3, SIDE, 2)),
            dma((8,)), dma((5,)),
        ],
        compiler_params=pltpu.CompilerParams(
            collective_id=0, has_side_effects=True, vmem_limit_bytes=limit
        ),
        name="layer",
    )(
        tokens, cotangent, counts.T, hops.T, offsets.T,
        norm_gain, qkv_weight, out_weight,
    )
    outs = pl.pallas_call(
        finish,
        out_shape=shapes,
        in_specs=[outside] * 5,
        out_specs=(outside,) * 5,
        scratch_shapes=[pltpu.VMEM(s.shape, s.dtype) for s in shapes] + [dma((2, 5))],
        compiler_params=pltpu.CompilerParams(vmem_limit_bytes=limit),
        name="finish",
    )(*outs)
    layer_out, input_grad, grad_qkv, grad_out, grad_gain = outs
    return (layer_out, input_grad, grad_qkv, grad_out, grad_gain.reshape(ROWS))


def solution(mesh):
    return jax.shard_map(
        body,
        mesh=mesh,
        in_specs=(P("dp", None), P("dp", None), P(), P(), P(), P(), P("dp", "rep"), P("dp", "rep")),
        out_specs=(P("dp", None), P("dp", None), P("dp", "rep"), P("dp", "rep"), P("dp")),
        check_vma=False,
    )
```
